32 devices in a mesh: patch: 16 (over z, y, core), head: 2 (over x).
Axes of the slice: x: 2, y: 2, z: 4, core: 2. Of those that a mesh axis runs over, the one named last changes fastest.
Arguments:
- fresh_q: bfloat16 [1536, 3072], P(('patch', 'head')), may hold values from -180 to 180
- fresh_k: bfloat16 [1536, 3072], P(('patch', 'head')), may hold values from -180 to 180
- fresh_v: bfloat16 [1536, 3072], P(('patch', 'head')), may hold values from -6 to 6
- stale_k: bfloat16 [1536, 3072], P('patch', 'head'), may hold values from -20 to 20
- stale_v: bfloat16 [1536, 3072], P('patch', 'head'), may hold values from -6 to 6
- q_gain: float32 [3072], replicated, may hold values from 0.1 to 1.9
- k_gain: float32 [3072], replicated, may hold values from 0.1 to 1.9
Outputs:
- attended: bfloat16 [1536, 3072], P(('patch', 'head'))
- key_cache: bfloat16 [1536, 3072], P('patch', 'head')
The draws below stay inside these ranges and needn't reach their ends.
All inputs are finite; a program needn't handle non-finite values.
Results may differ from the reference program's by a relative error of at most 0.011.
Values may be sent and summed in bfloat16 or wider, within the bound.
A program may use at most 192 MiB of HBM per device.

```python
import math
import jax
import jax.numpy as jnp
from jax import lax

HEADS = 24
HD = 128
TOK_PATCH = 96
TOKENS = 1536
N_PATCH = 16


def apply_scales(key, base_draw):
    subkeys = jax.random.split(key, 2)
    width_all = HEADS * HD
    row_scale = jnp.exp(jax.random.uniform(subkeys[0], (TOKENS, 1), jnp.float32, 0.0, math.log(10.0)))
    col_scale = jnp.exp(jax.random.uniform(subkeys[1], (1, width_all), jnp.float32, 0.0, math.log(10.0)))
    rising = 1.0 + 2.0 * (jnp.arange(width_all) // HD).astype(jnp.float32) / max(HEADS - 1, 1)
    return base_draw * row_scale * col_scale * rising[None, :] / 10.0


def draw_fresh_q(key, part):
    key = jax.random.fold_in(key, 11)
    subkeys = jax.random.split(key, 2)
    base_draw = jnp.clip(jax.random.normal(subkeys[0], (TOKENS, HEADS * HD), jnp.float32), -6.0, 6.0)
    drawn = apply_scales(subkeys[1], base_draw)
    return drawn.astype(jnp.bfloat16)


def draw_fresh_k(key, part):
    key = jax.random.fold_in(key, 12)
    subkeys = jax.random.split(key, 2)
    base_draw = jnp.clip(jax.random.normal(subkeys[0], (TOKENS, HEADS * HD), jnp.float32), -6.0, 6.0)
    return apply_scales(subkeys[1], base_draw).astype(jnp.bfloat16)


def draw_stale_k(key, part):
    key = jax.random.fold_in(key, 13)
    drawn = jnp.clip(jax.random.normal(key, (TOKENS, HEADS * HD), jnp.float32), -6.0, 6.0)
    return drawn.astype(jnp.bfloat16)


def level_of(stream_key, dims, cuts, least, high):
    factor_of, own = 1.0, jax.random.fold_in(stream_key, 6)
    for position, shards_of in cuts:
        draws = jnp.exp(jax.random.uniform(jax.random.fold_in(own, position), (shards_of,), jnp.float32, least / len(cuts), high / len(cuts)))
        factor_of = factor_of * jnp.repeat(draws, dims[position] // shards_of).reshape([-1 if axis == position else 1 for axis in range(len(dims))])
    return factor_of


def centred(key, extent, spread, bound, shards=(), kind=jnp.bfloat16):
    values = spread * jax.random.normal(key, extent, jnp.float32)
    if shards:
        values = values * level_of(key, extent, shards, -0.22, 0.18)
    return jnp.clip(values, -bound, bound).astype(kind)


def setup_inputs(seed: int = 0) -> dict:
    keys = jax.random.split(jax.random.key(seed), 8)
    fresh_q = draw_fresh_q(jax.random.fold_in(keys[7], 71), 0)
    fresh_k = draw_fresh_k(jax.random.fold_in(keys[7], 71), 0)
    fresh_v = centred(keys[2], (TOKENS, HEADS * HD), 1.0, 6.0, ((0, 32),))
    stale_k = draw_stale_k(jax.random.fold_in(keys[7], 71), 0)
    stale_v = centred(keys[4], (TOKENS, HEADS * HD), 1.0, 6.0, ((0, 16), (1, 2)))
    q_gain = jnp.clip(1.0 + 0.18 * jax.random.normal(keys[5], (HEADS * HD,), jnp.float32), 0.1, 1.9)
    k_gain = jnp.clip(1.0 + 0.18 * jax.random.normal(keys[6], (HEADS * HD,), jnp.float32), 0.1, 1.9)
    return dict(fresh_q=fresh_q, fresh_k=fresh_k, fresh_v=fresh_v, stale_k=stale_k, stale_v=stale_v, q_gain=q_gain, k_gain=k_gain)


EPSILON = 1e-06

def rms_rows(source, gain):
    values = source.astype(jnp.float32)
    mean_square = lax.optimization_barrier(jnp.mean(values * values, axis=1, keepdims=True))
    return (values * lax.rsqrt(mean_square + EPSILON) * gain.astype(jnp.float32)[None, :]).astype(jnp.bfloat16)

def reference(fresh_q, fresh_k, fresh_v, stale_k, stale_v, q_gain, k_gain):
    normed_q = rms_rows(fresh_q, q_gain)
    key_cache = rms_rows(fresh_k, k_gain)
    score_scale = HD ** (-0.5)

    def one_patch(patch_index):
        first_row = (patch_index * TOK_PATCH).astype(jnp.int32)
        queries = lax.dynamic_slice_in_dim(normed_q, first_row, TOK_PATCH, 0)
        own_keys = lax.dynamic_slice_in_dim(key_cache, first_row, TOK_PATCH, 0)
        own_values = lax.dynamic_slice_in_dim(fresh_v, first_row, TOK_PATCH, 0)
        key_rows = lax.dynamic_update_slice_in_dim(stale_k, own_keys, first_row, 0)
        value_rows = lax.dynamic_update_slice_in_dim(stale_v, own_values, first_row, 0)

        def one_head(head_index):
            first_col = (head_index * HD).astype(jnp.int32)
            query_head = lax.dynamic_slice_in_dim(queries, first_col, HD, 1)
            key_head = lax.dynamic_slice_in_dim(key_rows, first_col, HD, 1)
            value_head = lax.dynamic_slice_in_dim(value_rows, first_col, HD, 1)
            scores = jnp.dot(query_head, key_head.T, preferred_element_type=jnp.float32) * score_scale
            row_max = lax.optimization_barrier(jnp.max(scores, axis=1, keepdims=True))
            weights = jnp.exp(scores - row_max)
            row_sum = lax.optimization_barrier(jnp.sum(weights, axis=1, keepdims=True))
            mixed = jnp.dot(weights.astype(jnp.bfloat16), value_head, preferred_element_type=jnp.float32)
            return (mixed / row_sum).astype(jnp.bfloat16)
        per_head = lax.map(one_head, jnp.arange(HEADS, dtype=jnp.int32))
        return jnp.transpose(per_head, (1, 0, 2)).reshape(TOK_PATCH, HEADS * HD)
    attended = lax.map(one_patch, jnp.arange(N_PATCH, dtype=jnp.int32))
    return (attended.reshape(TOKENS, HEADS * HD), key_cache)
```

```python
import jax
import jax.numpy as jnp
from jax import lax
from jax.experimental import pallas as pl
from jax.experimental.pallas import tpu as pltpu
from jax.sharding import PartitionSpec as P

HEADS = 24
HD = 128


EPSILON = 1e-06
LOWEST = -1e30


def scale_rows(source, square_sum, gain, width_all):
    values = source.astype(jnp.float32)
    factor = lax.rsqrt(square_sum[:, None] / width_all + EPSILON)
    return (values * factor * gain[None, :]).astype(jnp.bfloat16)


def heads_view(source, heads_dev):
    return source.reshape(source.shape[0], heads_dev, source.shape[1] // heads_dev)


def scaled_scores(queries, key_rows):
    score_scale = HD ** (-0.5)
    return (
        jnp.einsum("qhe,khe->hqk", queries, key_rows, preferred_element_type=jnp.float32)
        * score_scale
    )


def block_stats(scores, value_rows):
    row_max = jnp.max(scores, axis=2)
    weights = jnp.exp(scores - row_max[:, :, None])
    row_sum = jnp.sum(weights, axis=2)
    weighted = jnp.einsum(
        "hqk,khe->hqe", weights.astype(jnp.bfloat16), value_rows, preferred_element_type=jnp.float32
    )
    return (row_max, row_sum, weighted)


def absorb(carried, scores, value_rows):
    row_max, row_sum, weighted = carried
    new_max = jnp.maximum(row_max, jnp.max(scores, axis=2))
    rescale = jnp.exp(row_max - new_max)
    weights = jnp.exp(scores - new_max[:, :, None])
    row_sum = row_sum * rescale + jnp.sum(weights, axis=2)
    added = jnp.einsum(
        "hqk,khe->hqe", weights.astype(jnp.bfloat16), value_rows, preferred_element_type=jnp.float32
    )
    return (new_max, row_sum, weighted * rescale[:, :, None] + added)


def body(fresh_q, fresh_k, fresh_v, stale_k, stale_v, q_gain, k_gain):
    groups = lax.axis_size("head")
    heads_dev = HEADS // groups
    width_dev = heads_dev * HD
    width_all = q_gain.shape[0]
    local_q, local_k, local_v = (
        lax.all_to_all(fresh_q, "head", split_axis=1, concat_axis=0, tiled=True),
        lax.all_to_all(fresh_k, "head", split_axis=1, concat_axis=0, tiled=True),
        lax.all_to_all(fresh_v, "head", split_axis=1, concat_axis=0, tiled=True),
    )
    first_col = lax.axis_index("head") * width_dev
    gain_q = lax.dynamic_slice_in_dim(q_gain, first_col, width_dev, 0)
    gain_k = lax.dynamic_slice_in_dim(k_gain, first_col, width_dev, 0)
    squares_q = jnp.sum(jnp.square(local_q.astype(jnp.float32)), axis=1)
    squares_k = jnp.sum(jnp.square(local_k.astype(jnp.float32)), axis=1)
    total_q, total_k = lax.psum((squares_q, squares_k), "head")
    normed_q = scale_rows(local_q, total_q, gain_q, width_all)
    key_cache = scale_rows(local_k, total_k, gain_k, width_all)
    patch_rows = normed_q.shape[0]
    my_patch = lax.axis_index("patch")
    query_view = heads_view(normed_q, heads_dev)
    fresh_state = block_stats(
        scaled_scores(query_view, heads_view(key_cache, heads_dev)), heads_view(local_v, heads_dev)
    )
    segment = (
        lax.all_gather(stale_k, "patch", axis=0, tiled=True),
        lax.all_gather(stale_v, "patch", axis=0, tiled=True),
    )
    key_rows = heads_view(segment[0], heads_dev)
    value_rows = heads_view(segment[1], heads_dev)
    scores = scaled_scores(query_view, key_rows)
    owner_patch = jnp.arange(segment[0].shape[0], dtype=jnp.int32) // patch_rows
    scores = jnp.where((owner_patch == my_patch)[None, None, :], 2.0 * LOWEST, scores)
    folded = absorb(fresh_state, scores, value_rows)
    row_max, row_sum, weighted = folded
    result = (weighted / row_sum[:, :, None]).astype(jnp.bfloat16)
    result = jnp.transpose(result, (1, 0, 2)).reshape(patch_rows, width_dev)
    attended = lax.all_to_all(result, "head", split_axis=0, concat_axis=1, tiled=True)
    return (attended, key_cache)

SPLIT = 4
MESH_TYPE = pl.DeviceIdType.MESH


def rms_rows(source, gain):
    values = source.astype(jnp.float32)
    mean_square = jnp.mean(values * values, axis=1, keepdims=True)
    return (values * lax.rsqrt(mean_square + EPSILON) * gain).astype(jnp.bfloat16)


def kernel(
    fresh_q, fresh_k, fresh_v, stale_k, stale_v, q_gain, k_gain,
    attended, key_cache,
    normed_q, normed_k, q_rows, fresh_k_rows, fresh_v_rows, k_rows, v_rows, result,
    fresh_send, fresh_recv, stale_send, stale_recv, pass_send, pass_recv,
    out_send, out_recv, cache_send, cache_recv, local_sem,
):
    half_rows = fresh_q.shape[0]
    patch_rows, width_dev = stale_k.shape
    width = width_dev // SPLIT
    heads = width // HD
    chunk = SPLIT * patch_rows

    patch, x = lax.axis_index("patch"), lax.axis_index("head")
    core, y = lax.rem(patch, 2), lax.rem(patch // 2, 2)
    low, high = lax.rem(patch // 4, 2), patch // 8

    def flip(bit, by):
        return lax.rem(bit + by, 2)

    def patch_at(by_high, by_low, by_y, by_core=0):
        return flip(high, by_high) * 8 + flip(low, by_low) * 4 + flip(y, by_y) * 2 + flip(core, by_core)

    def group_at(by_low, by_y):
        return flip(low, by_low) * 2 + flip(y, by_y)

    def rows_of(index, size):
        return pl.ds(pl.multiple_of(index * size, size), size)

    def columns_of(index):
        return pl.ds(pl.multiple_of(index * width, width), width)

    cube = [(dx, dl, dy) for dx in range(2) for dl in range(2) for dy in range(2)]
    plane = [(dh, dl, dy) for dh in range(2) for dl in range(2) for dy in range(2)]
    sibling = (patch_at(0, 0, 0, 1), x)

    barrier = pltpu.get_barrier_semaphore()
    partners = [(patch_at(0, dl, dy), flip(x, dx)) for dx, dl, dy in cube[1:]]
    partners += [(patch_at(1, dl, dy), x) for dh, dl, dy in plane[4:]]
    partners += [sibling]
    for partner in partners:
        pl.semaphore_signal(barrier, inc=1, device_id=partner, device_id_type=MESH_TYPE)

    normed_q[...] = rms_rows(fresh_q[...], q_gain[...])
    normed_k[...] = rms_rows(fresh_k[...], k_gain[...])
    pl.semaphore_wait(barrier, len(partners))

    started, local = [], []

    def send(source, target, send_sem, recv_sem, device):
        copy = pltpu.make_async_remote_copy(
            src_ref=source, dst_ref=target, send_sem=send_sem, recv_sem=recv_sem,
            device_id=device, device_id_type=MESH_TYPE,
        )
        copy.start()
        started.append(copy)

    def arrive(target, send_sem, recv_sem, device):
        pltpu.make_async_remote_copy(
            src_ref=target, dst_ref=target, send_sem=send_sem, recv_sem=recv_sem,
            device_id=device, device_id_type=MESH_TYPE,
        ).wait_recv()

    def place(source, target):
        copy = pltpu.make_async_copy(source, target, local_sem.at[len(local)])
        copy.start()
        local.append(copy)
        return copy

    my_rows = rows_of(group_at(0, 0) * 2 + x, half_rows)
    my_columns = columns_of(x * SPLIT + group_at(0, 0))
    fresh = [(normed_q, q_rows), (normed_k, fresh_k_rows), (fresh_v, fresh_v_rows)]
    stale = [(stale_k, k_rows), (stale_v, v_rows)]

    def send_fresh(t):
        source, target = fresh[t]
        for i, (dx, dl, dy) in enumerate(cube):
            columns = columns_of(flip(x, dx) * SPLIT + group_at(dl, dy))
            if i == 0:
                place(source.at[:, columns], target.at[my_rows])
            else:
                send(
                    source.at[:, columns], target.at[my_rows],
                    fresh_send.at[t, i], fresh_recv.at[t, i],
                    (patch_at(0, dl, dy), flip(x, dx)),
                )

    def send_stale(i):
        dh, dl, dy = plane[i]
        rows = rows_of(patch, patch_rows)
        for t, (source, target) in enumerate(stale):
            block = source.at[:, columns_of(group_at(dl, dy))]
            if i == 0:
                place(block, target.at[rows])
                send(block, target.at[rows], pass_send.at[t, 0], pass_recv.at[t, 0], sibling)
            else:
                send(
                    block, target.at[rows], stale_send.at[t, i], stale_recv.at[t, i],
                    (patch_at(dh, dl, dy), x),
                )

    send_fresh(0)
    for i in range(4, 8):
        send_stale(i)
    send_fresh(1)
    send_fresh(2)
    for i in range(4):
        send_stale(i)
    cache_rows = rows_of(x, half_rows)
    side = pl.ds(pl.multiple_of(x * width_dev, width_dev), width_dev)
    other_side = pl.ds(pl.multiple_of((1 - x) * width_dev, width_dev), width_dev)
    place(normed_k.at[:, side], key_cache.at[cache_rows])
    send(
        normed_k.at[:, other_side], key_cache.at[cache_rows],
        cache_send.at[0], cache_recv.at[0], (patch, 1 - x),
    )
    for copy in local:
        copy.wait()

    for t, (_, target) in enumerate(fresh):
        for i, (dx, dl, dy) in enumerate(cube):
            if i > 0:
                arrive(
                    target.at[rows_of(group_at(dl, dy) * 2 + flip(x, dx), half_rows)],
                    fresh_send.at[t, i], fresh_recv.at[t, i],
                    (patch_at(0, dl, dy), flip(x, dx)),
                )

    factor = HD ** (-0.5) * 1.4426950408889634
    state = [None] * heads
    row_patch = lax.broadcasted_iota(jnp.int32, (chunk, 1), 0) // patch_rows
    column_patch = lax.broadcasted_iota(jnp.int32, (1, chunk), 1) // patch_rows

    def attend(h, keys, values, masked):
        columns = slice(h * HD, (h + 1) * HD)
        scores = lax.dot_general(
            q_rows[:, columns], keys[:, columns], (((1,), (1,)), ((), ())),
            preferred_element_type=jnp.float32,
        )
        if masked is not None:
            scores = jnp.where(masked, 2.0 * LOWEST, scores)
        new_max = jnp.max(scores, axis=1, keepdims=True)
        if state[h] is not None:
            row_max, row_sum, weighted = state[h]
            new_max = jnp.maximum(row_max, new_max)
        weights = jnp.exp2((scores - new_max) * factor)
        new_sum = jnp.sum(weights, axis=1, keepdims=True)
        added = jnp.dot(
            weights.astype(jnp.bfloat16), values[:, columns], preferred_element_type=jnp.float32
        )
        if state[h] is not None:
            rescale = jnp.exp2((row_max - new_max) * factor)
            new_sum += row_sum * rescale
            added += weighted * rescale
        state[h] = (new_max, new_sum, added)

    for h in range(heads):
        attend(h, fresh_k_rows, fresh_v_rows, row_patch != column_patch)

    for dh, dl in ((0, 0), (0, 1), (1, 0), (1, 1)):
        indices = [i for i in range(8) if plane[i][:2] == (dh, dl)]
        for i in indices:
            rows = rows_of(patch_at(*plane[i]), patch_rows)
            for t, (_, target) in enumerate(stale):
                if i > 0:
                    arrive(
                        target.at[rows], stale_send.at[t, i], stale_recv.at[t, i],
                        (patch_at(*plane[i]), x),
                    )
                    send(
                        target.at[rows], target.at[rows],
                        pass_send.at[t, i], pass_recv.at[t, i], sibling,
                    )
        for i in indices:
            rows = rows_of(patch_at(*plane[i], 1), patch_rows)
            for t, (_, target) in enumerate(stale):
                arrive(target.at[rows], pass_send.at[t, i], pass_recv.at[t, i], sibling)
        block = rows_of(flip(high, dh) * 2 + flip(low, dl), chunk)
        masked = None
        if dh == 0:
            key_patch = column_patch + flip(low, dl) * 4
            masked = row_patch * 2 + core == key_patch
        for h in range(heads):
            attend(h, k_rows.at[block], v_rows.at[block], masked)

    for h in range(heads):
        _, row_sum, weighted = state[h]
        result[:, h * HD : (h + 1) * HD] = (weighted / row_sum).astype(jnp.bfloat16)

    last = None
    for i, (dx, dl, dy) in enumerate(cube):
        rows = rows_of(group_at(dl, dy) * 2 + flip(x, dx), half_rows)
        if i == 0:
            last = place(result.at[rows], attended.at[:, my_columns])
        else:
            send(
                result.at[rows], attended.at[:, my_columns], out_send.at[i], out_recv.at[i],
                (patch_at(0, dl, dy), flip(x, dx)),
            )
    arrive(key_cache.at[rows_of(1 - x, half_rows)], cache_send.at[0], cache_recv.at[0], (patch, 1 - x))
    for i, (dx, dl, dy) in enumerate(cube):
        if i > 0:
            arrive(
                attended.at[:, columns_of(flip(x, dx) * SPLIT + group_at(dl, dy))],
                out_send.at[i], out_recv.at[i], (patch_at(0, dl, dy), flip(x, dx)),
            )
    last.wait()
    for copy in started:
        copy.wait_send()


def kernel_body(fresh_q, fresh_k, fresh_v, stale_k, stale_v, q_gain, k_gain):
    half_rows, width_all = fresh_q.shape
    patch_rows, width_dev = stale_k.shape
    tokens = patch_rows * lax.axis_size("patch")
    width = width_dev // SPLIT
    group = (SPLIT * patch_rows, width)
    bf16 = jnp.bfloat16
    in_vmem = pl.BlockSpec(memory_space=pltpu.VMEM)
    anywhere = pl.BlockSpec(memory_space=pl.ANY)
    sems = [(3, 8), (3, 8), (2, 8), (2, 8), (2, 8), (2, 8), (8,), (8,), (1,), (1,), (7,)]
    pairs = (width_dev // HD) * patch_rows * tokens
    return pl.pallas_call(
        kernel,
        out_shape=[
            jax.ShapeDtypeStruct((half_rows, width_all), bf16),
            jax.ShapeDtypeStruct((patch_rows, width_dev), bf16),
        ],
        in_specs=[in_vmem, in_vmem, anywhere, anywhere, anywhere, in_vmem, in_vmem],
        out_specs=[anywhere, anywhere],
        scratch_shapes=[
            pltpu.VMEM((half_rows, width_all), bf16),
            pltpu.VMEM((half_rows, width_all), bf16),
            pltpu.VMEM(group, bf16),
            pltpu.VMEM(group, bf16),
            pltpu.VMEM(group, bf16),
            pltpu.VMEM((tokens, width), bf16),
            pltpu.VMEM((tokens, width), bf16),
            pltpu.VMEM(group, bf16),
        ]
        + [pltpu.SemaphoreType.DMA(shape) for shape in sems],
        compiler_params=pltpu.CompilerParams(
            collective_id=0, has_side_effects=True, vmem_limit_bytes=40 * 1024 * 1024
        ),
        cost_estimate=pl.CostEstimate(
            flops=4 * pairs * HD, bytes_accessed=8 * tokens * width, transcendentals=pairs
        ),
    )(fresh_q, fresh_k, fresh_v, stale_k, stale_v, q_gain[None, :], k_gain[None, :])


def solution(mesh):
    placed = (
        P(("patch", "head"), None),
        P(("patch", "head"), None),
        P(("patch", "head"), None),
        P("patch", "head"),
        P("patch", "head"),
        P(),
        P(),
    )
    fits = mesh.shape["patch"] == 16 and mesh.shape["head"] == 2
    return jax.shard_map(
        kernel_body if fits else body,
        mesh=mesh,
        in_specs=placed,
        out_specs=(P(("patch", "head"), None), P("patch", "head")),
        check_vma=False,
    )
```

```python
import jax
import jax.numpy as jnp
from jax import lax
from jax.experimental import pallas as pl
from jax.experimental.pallas import tpu as pltpu
from jax.sharding import PartitionSpec as P

HEADS = 24
HD = 128


EPSILON = 1e-06
LOWEST = -1e30


def scale_rows(source, square_sum, gain, width_all):
    values = source.astype(jnp.float32)
    factor = lax.rsqrt(square_sum[:, None] / width_all + EPSILON)
    return (values * factor * gain[None, :]).astype(jnp.bfloat16)


def heads_view(source, heads_dev):
    return source.reshape(source.shape[0], heads_dev, source.shape[1] // heads_dev)


def scaled_scores(queries, key_rows):
    score_scale = HD ** (-0.5)
    return (
        jnp.einsum("qhe,khe->hqk", queries, key_rows, preferred_element_type=jnp.float32)
        * score_scale
    )


def block_stats(scores, value_rows):
    row_max = jnp.max(scores, axis=2)
    weights = jnp.exp(scores - row_max[:, :, None])
    row_sum = jnp.sum(weights, axis=2)
    weighted = jnp.einsum(
        "hqk,khe->hqe", weights.astype(jnp.bfloat16), value_rows, preferred_element_type=jnp.float32
    )
    return (row_max, row_sum, weighted)


def absorb(carried, scores, value_rows):
    row_max, row_sum, weighted = carried
    new_max = jnp.maximum(row_max, jnp.max(scores, axis=2))
    rescale = jnp.exp(row_max - new_max)
    weights = jnp.exp(scores - new_max[:, :, None])
    row_sum = row_sum * rescale + jnp.sum(weights, axis=2)
    added = jnp.einsum(
        "hqk,khe->hqe", weights.astype(jnp.bfloat16), value_rows, preferred_element_type=jnp.float32
    )
    return (new_max, row_sum, weighted * rescale[:, :, None] + added)


def body(fresh_q, fresh_k, fresh_v, stale_k, stale_v, q_gain, k_gain):
    groups = lax.axis_size("head")
    heads_dev = HEADS // groups
    width_dev = heads_dev * HD
    width_all = q_gain.shape[0]
    local_q, local_k, local_v = (
        lax.all_to_all(fresh_q, "head", split_axis=1, concat_axis=0, tiled=True),
        lax.all_to_all(fresh_k, "head", split_axis=1, concat_axis=0, tiled=True),
        lax.all_to_all(fresh_v, "head", split_axis=1, concat_axis=0, tiled=True),
    )
    first_col = lax.axis_index("head") * width_dev
    gain_q = lax.dynamic_slice_in_dim(q_gain, first_col, width_dev, 0)
    gain_k = lax.dynamic_slice_in_dim(k_gain, first_col, width_dev, 0)
    squares_q = jnp.sum(jnp.square(local_q.astype(jnp.float32)), axis=1)
    squares_k = jnp.sum(jnp.square(local_k.astype(jnp.float32)), axis=1)
    total_q, total_k = lax.psum((squares_q, squares_k), "head")
    normed_q = scale_rows(local_q, total_q, gain_q, width_all)
    key_cache = scale_rows(local_k, total_k, gain_k, width_all)
    patch_rows = normed_q.shape[0]
    my_patch = lax.axis_index("patch")
    query_view = heads_view(normed_q, heads_dev)
    fresh_state = block_stats(
        scaled_scores(query_view, heads_view(key_cache, heads_dev)), heads_view(local_v, heads_dev)
    )
    segment = (
        lax.all_gather(stale_k, "patch", axis=0, tiled=True),
        lax.all_gather(stale_v, "patch", axis=0, tiled=True),
    )
    key_rows = heads_view(segment[0], heads_dev)
    value_rows = heads_view(segment[1], heads_dev)
    scores = scaled_scores(query_view, key_rows)
    owner_patch = jnp.arange(segment[0].shape[0], dtype=jnp.int32) // patch_rows
    scores = jnp.where((owner_patch == my_patch)[None, None, :], 2.0 * LOWEST, scores)
    folded = absorb(fresh_state, scores, value_rows)
    row_max, row_sum, weighted = folded
    result = (weighted / row_sum[:, :, None]).astype(jnp.bfloat16)
    result = jnp.transpose(result, (1, 0, 2)).reshape(patch_rows, width_dev)
    attended = lax.all_to_all(result, "head", split_axis=0, concat_axis=1, tiled=True)
    return (attended, key_cache)

SPLIT = 4
MESH_TYPE = pl.DeviceIdType.MESH


def rms_rows(source, gain):
    values = source.astype(jnp.float32)
    mean_square = jnp.mean(values * values, axis=1, keepdims=True)
    return (values * lax.rsqrt(mean_square + EPSILON) * gain).astype(jnp.bfloat16)


def kernel(
    fresh_q, fresh_k, fresh_v, stale_k, stale_v, q_gain, k_gain,
    attended, key_cache,
    raw_q, raw_k, gains, normed_q, normed_k, q_rows, fresh_k_rows, fresh_v_rows, k_rows, v_rows, result,
    fresh_send, fresh_recv, stale_send, stale_recv, pass_send, pass_recv,
    out_send, out_recv, cache_send, cache_recv, local_sem,
):
    half_rows = fresh_q.shape[0]
    patch_rows, width_dev = stale_k.shape
    width = width_dev // SPLIT
    heads = width // HD
    chunk = SPLIT * patch_rows

    patch, x = lax.axis_index("patch"), lax.axis_index("head")
    core, y = lax.rem(patch, 2), lax.rem(patch // 2, 2)
    low, high = lax.rem(patch // 4, 2), patch // 8

    def flip(bit, by):
        return lax.rem(bit + by, 2)

    def patch_at(by_high, by_low, by_y, by_core=0):
        return flip(high, by_high) * 8 + flip(low, by_low) * 4 + flip(y, by_y) * 2 + flip(core, by_core)

    def group_at(by_low, by_y):
        return flip(low, by_low) * 2 + flip(y, by_y)

    def rows_of(index, size):
        return pl.ds(pl.multiple_of(index * size, size), size)

    def columns_of(index):
        return pl.ds(pl.multiple_of(index * width, width), width)

    def head_columns(dx, dl, dy, h):
        first = (flip(x, dx) * SPLIT + group_at(dl, dy)) * width + h * HD
        return pl.ds(pl.multiple_of(first, HD), HD)

    cube = [(dx, dl, dy) for dx in range(2) for dl in range(2) for dy in range(2)]
    plane = [(dh, dl, dy) for dh in range(2) for dl in range(2) for dy in range(2)]
    sibling = (patch_at(0, 0, 0, 1), x)

    barrier = pltpu.get_barrier_semaphore()
    partners = [(patch_at(0, dl, dy), flip(x, dx)) for dx, dl, dy in cube[1:]]
    partners += [(patch_at(1, dl, dy), x) for dh, dl, dy in plane[4:]]
    partners += [sibling]
    for partner in partners:
        pl.semaphore_signal(barrier, inc=1, device_id=partner, device_id_type=MESH_TYPE)

    started, local = [], []

    def send(source, target, send_sem, recv_sem, device):
        copy = pltpu.make_async_remote_copy(
            src_ref=source, dst_ref=target, send_sem=send_sem, recv_sem=recv_sem,
            device_id=device, device_id_type=MESH_TYPE,
        )
        copy.start()
        started.append(copy)

    def arrive(target, send_sem, recv_sem, device):
        pltpu.make_async_remote_copy(
            src_ref=target, dst_ref=target, send_sem=send_sem, recv_sem=recv_sem,
            device_id=device, device_id_type=MESH_TYPE,
        ).wait_recv()

    def place(source, target):
        copy = pltpu.make_async_copy(source, target, local_sem.at[len(local)])
        copy.start()
        local.append(copy)
        return copy

    place(fresh_q, raw_q)
    place(fresh_k, raw_k)
    place(q_gain, gains.at[0])
    place(k_gain, gains.at[1])
    pl.semaphore_wait(barrier, len(partners))

    my_rows = rows_of(group_at(0, 0) * 2 + x, half_rows)
    fresh = [(normed_q, q_rows), (normed_k, fresh_k_rows), (fresh_v, fresh_v_rows)]
    stale = [(stale_k, k_rows), (stale_v, v_rows)]

    def send_fresh(t):
        source, target = fresh[t]
        for i, (dx, dl, dy) in enumerate(cube):
            columns = columns_of(flip(x, dx) * SPLIT + group_at(dl, dy))
            if i == 0:
                place(source.at[:, columns], target.at[my_rows])
            else:
                send(
                    source.at[:, columns], target.at[my_rows],
                    fresh_send.at[t, i], fresh_recv.at[t, i],
                    (patch_at(0, dl, dy), flip(x, dx)),
                )

    def send_stale(i):
        dh, dl, dy = plane[i]
        rows = rows_of(patch, patch_rows)
        for t, (source, target) in enumerate(stale):
            block = source.at[:, columns_of(group_at(dl, dy))]
            if i == 0:
                place(block, target.at[rows])
                send(block, target.at[rows], pass_send.at[t, 0], pass_recv.at[t, 0], sibling)
            else:
                send(
                    block, target.at[rows], stale_send.at[t, i], stale_recv.at[t, i],
                    (patch_at(dh, dl, dy), x),
                )

    for i in range(4, 8):
        send_stale(i)
    send_fresh(2)
    for copy in local[:4]:
        copy.wait()
    normed_q[...] = rms_rows(raw_q[...], gains[0])
    send_fresh(0)
    normed_k[...] = rms_rows(raw_k[...], gains[1])
    send_fresh(1)
    for i in range(4):
        send_stale(i)
    cache_rows = rows_of(x, half_rows)
    side = pl.ds(pl.multiple_of(x * width_dev, width_dev), width_dev)
    other_side = pl.ds(pl.multiple_of((1 - x) * width_dev, width_dev), width_dev)
    place(normed_k.at[:, side], key_cache.at[cache_rows])
    send(
        normed_k.at[:, other_side], key_cache.at[cache_rows],
        cache_send.at[0], cache_recv.at[0], (patch, 1 - x),
    )
    for copy in local[4:]:
        copy.wait()

    for t, (_, target) in enumerate(fresh):
        for i, (dx, dl, dy) in enumerate(cube):
            if i > 0:
                arrive(
                    target.at[rows_of(group_at(dl, dy) * 2 + flip(x, dx), half_rows)],
                    fresh_send.at[t, i], fresh_recv.at[t, i],
                    (patch_at(0, dl, dy), flip(x, dx)),
                )

    factor = HD ** (-0.5) * 1.4426950408889634
    state = [None] * heads
    row_patch = lax.broadcasted_iota(jnp.int32, (chunk, 1), 0) // patch_rows
    column_patch = lax.broadcasted_iota(jnp.int32, (1, chunk), 1) // patch_rows

    def attend(h, keys, values, masked):
        columns = slice(h * HD, (h + 1) * HD)
        scores = lax.dot_general(
            q_rows[:, columns], keys[:, columns], (((1,), (1,)), ((), ())),
            preferred_element_type=jnp.float32,
        )
        if masked is not None:
            scores = jnp.where(masked, 2.0 * LOWEST, scores)
        new_max = jnp.max(scores, axis=1, keepdims=True)
        if state[h] is not None:
            row_max, row_sum, weighted = state[h]
            new_max = jnp.maximum(row_max, new_max)
        weights = jnp.exp2((scores - new_max) * factor)
        new_sum = jnp.sum(weights, axis=1, keepdims=True)
        added = jnp.dot(
            weights.astype(jnp.bfloat16), values[:, columns], preferred_element_type=jnp.float32
        )
        if state[h] is not None:
            rescale = jnp.exp2((row_max - new_max) * factor)
            new_sum += row_sum * rescale
            added += weighted * rescale
        state[h] = (new_max, new_sum, added)

    def give_back(h):
        _, row_sum, weighted = state[h]
        columns = slice(h * HD, (h + 1) * HD)
        result[:, columns] = (weighted / row_sum).astype(jnp.bfloat16)
        for i, (dx, dl, dy) in enumerate(cube):
            block = result.at[rows_of(group_at(dl, dy) * 2 + flip(x, dx), half_rows), columns]
            target = attended.at[:, head_columns(0, 0, 0, h)]
            if i == 0:
                place(block, target)
            else:
                send(
                    block, target, out_send.at[h, i], out_recv.at[h, i],
                    (patch_at(0, dl, dy), flip(x, dx)),
                )

    for h in range(heads):
        attend(h, fresh_k_rows, fresh_v_rows, row_patch != column_patch)

    for dh, dl in ((1, 0), (1, 1), (0, 0), (0, 1)):
        indices = [i for i in range(8) if plane[i][:2] == (dh, dl)]
        for i in indices:
            rows = rows_of(patch_at(*plane[i]), patch_rows)
            for t, (_, target) in enumerate(stale):
                if i > 0:
                    arrive(
                        target.at[rows], stale_send.at[t, i], stale_recv.at[t, i],
                        (patch_at(*plane[i]), x),
                    )
                    send(
                        target.at[rows], target.at[rows],
                        pass_send.at[t, i], pass_recv.at[t, i], sibling,
                    )
        for i in indices:
            rows = rows_of(patch_at(*plane[i], 1), patch_rows)
            for t, (_, target) in enumerate(stale):
                arrive(target.at[rows], pass_send.at[t, i], pass_recv.at[t, i], sibling)
        block = rows_of(flip(high, dh) * 2 + flip(low, dl), chunk)
        masked = None
        if dh == 0:
            key_patch = column_patch + flip(low, dl) * 4
            masked = row_patch * 2 + core == key_patch
        for h in range(heads):
            attend(h, k_rows.at[block], v_rows.at[block], masked)
            if (dh, dl) == (0, 1):
                give_back(h)

    arrive(key_cache.at[rows_of(1 - x, half_rows)], cache_send.at[0], cache_recv.at[0], (patch, 1 - x))
    for h in range(heads):
        for i, (dx, dl, dy) in enumerate(cube):
            if i > 0:
                arrive(
                    attended.at[:, head_columns(dx, dl, dy, h)],
                    out_send.at[h, i], out_recv.at[h, i], (patch_at(0, dl, dy), flip(x, dx)),
                )
    for copy in local[-heads:]:
        copy.wait()
    for copy in started:
        copy.wait_send()


def kernel_body(fresh_q, fresh_k, fresh_v, stale_k, stale_v, q_gain, k_gain):
    half_rows, width_all = fresh_q.shape
    patch_rows, width_dev = stale_k.shape
    tokens = patch_rows * lax.axis_size("patch")
    width = width_dev // SPLIT
    group = (SPLIT * patch_rows, width)
    bf16 = jnp.bfloat16
    in_hbm = pl.BlockSpec(memory_space=pltpu.HBM)
    sems = [(3, 8), (3, 8), (2, 8), (2, 8), (2, 8), (2, 8)]
    heads = width // HD
    sems += [(heads, 8), (heads, 8), (1,), (1,), (10 + heads,)]
    pairs = (width_dev // HD) * patch_rows * tokens
    return pl.pallas_call(
        kernel,
        out_shape=[
            jax.ShapeDtypeStruct((half_rows, width_all), bf16),
            jax.ShapeDtypeStruct((patch_rows, width_dev), bf16),
        ],
        in_specs=[in_hbm] * 7,
        out_specs=[in_hbm] * 2,
        scratch_shapes=[
            pltpu.VMEM((half_rows, width_all), bf16),
            pltpu.VMEM((half_rows, width_all), bf16),
            pltpu.VMEM((2, 1, width_all), jnp.float32),
            pltpu.VMEM((half_rows, width_all), bf16),
            pltpu.VMEM((half_rows, width_all), bf16),
            pltpu.VMEM(group, bf16),
            pltpu.VMEM(group, bf16),
            pltpu.VMEM(group, bf16),
            pltpu.VMEM((tokens, width), bf16),
            pltpu.VMEM((tokens, width), bf16),
            pltpu.VMEM(group, bf16),
        ]
        + [pltpu.SemaphoreType.DMA(shape) for shape in sems],
        compiler_params=pltpu.CompilerParams(
            collective_id=0, has_side_effects=True, vmem_limit_bytes=62 * 1024 * 1024
        ),
        cost_estimate=pl.CostEstimate(
            flops=4 * pairs * HD, bytes_accessed=8 * tokens * width, transcendentals=pairs
        ),
    )(fresh_q, fresh_k, fresh_v, stale_k, stale_v, q_gain[None, :], k_gain[None, :])


def solution(mesh):
    placed = (
        P(("patch", "head"), None),
        P(("patch", "head"), None),
        P(("patch", "head"), None),
        P("patch", "head"),
        P("patch", "head"),
        P(),
        P(),
    )
    fits = mesh.shape["patch"] == 16 and mesh.shape["head"] == 2
    return jax.shard_map(
        kernel_body if fits else body,
        mesh=mesh,
        in_specs=placed,
        out_specs=(P(("patch", "head"), None), P("patch", "head")),
        check_vma=False,
    )
```

```python
import jax
import jax.numpy as jnp
from jax import lax
from jax.experimental import pallas as pl
from jax.experimental.pallas import tpu as pltpu
from jax.sharding import PartitionSpec as P

HEADS = 24
HD = 128


EPSILON = 1e-06
LOWEST = -1e30


def scale_rows(source, square_sum, gain, width_all):
    values = source.astype(jnp.float32)
    factor = lax.rsqrt(square_sum[:, None] / width_all + EPSILON)
    return (values * factor * gain[None, :]).astype(jnp.bfloat16)


def heads_view(source, heads_dev):
    return source.reshape(source.shape[0], heads_dev, source.shape[1] // heads_dev)


def scaled_scores(queries, key_rows):
    score_scale = HD ** (-0.5)
    return (
        jnp.einsum("qhe,khe->hqk", queries, key_rows, preferred_element_type=jnp.float32)
        * score_scale
    )


def block_stats(scores, value_rows):
    row_max = jnp.max(scores, axis=2)
    weights = jnp.exp(scores - row_max[:, :, None])
    row_sum = jnp.sum(weights, axis=2)
    weighted = jnp.einsum(
        "hqk,khe->hqe", weights.astype(jnp.bfloat16), value_rows, preferred_element_type=jnp.float32
    )
    return (row_max, row_sum, weighted)


def absorb(carried, scores, value_rows):
    row_max, row_sum, weighted = carried
    new_max = jnp.maximum(row_max, jnp.max(scores, axis=2))
    rescale = jnp.exp(row_max - new_max)
    weights = jnp.exp(scores - new_max[:, :, None])
    row_sum = row_sum * rescale + jnp.sum(weights, axis=2)
    added = jnp.einsum(
        "hqk,khe->hqe", weights.astype(jnp.bfloat16), value_rows, preferred_element_type=jnp.float32
    )
    return (new_max, row_sum, weighted * rescale[:, :, None] + added)


def body(fresh_q, fresh_k, fresh_v, stale_k, stale_v, q_gain, k_gain):
    groups = lax.axis_size("head")
    heads_dev = HEADS // groups
    width_dev = heads_dev * HD
    width_all = q_gain.shape[0]
    local_q, local_k, local_v = (
        lax.all_to_all(fresh_q, "head", split_axis=1, concat_axis=0, tiled=True),
        lax.all_to_all(fresh_k, "head", split_axis=1, concat_axis=0, tiled=True),
        lax.all_to_all(fresh_v, "head", split_axis=1, concat_axis=0, tiled=True),
    )
    first_col = lax.axis_index("head") * width_dev
    gain_q = lax.dynamic_slice_in_dim(q_gain, first_col, width_dev, 0)
    gain_k = lax.dynamic_slice_in_dim(k_gain, first_col, width_dev, 0)
    squares_q = jnp.sum(jnp.square(local_q.astype(jnp.float32)), axis=1)
    squares_k = jnp.sum(jnp.square(local_k.astype(jnp.float32)), axis=1)
    total_q, total_k = lax.psum((squares_q, squares_k), "head")
    normed_q = scale_rows(local_q, total_q, gain_q, width_all)
    key_cache = scale_rows(local_k, total_k, gain_k, width_all)
    patch_rows = normed_q.shape[0]
    my_patch = lax.axis_index("patch")
    query_view = heads_view(normed_q, heads_dev)
    fresh_state = block_stats(
        scaled_scores(query_view, heads_view(key_cache, heads_dev)), heads_view(local_v, heads_dev)
    )
    segment = (
        lax.all_gather(stale_k, "patch", axis=0, tiled=True),
        lax.all_gather(stale_v, "patch", axis=0, tiled=True),
    )
    key_rows = heads_view(segment[0], heads_dev)
    value_rows = heads_view(segment[1], heads_dev)
    scores = scaled_scores(query_view, key_rows)
    owner_patch = jnp.arange(segment[0].shape[0], dtype=jnp.int32) // patch_rows
    scores = jnp.where((owner_patch == my_patch)[None, None, :], 2.0 * LOWEST, scores)
    folded = absorb(fresh_state, scores, value_rows)
    row_max, row_sum, weighted = folded
    result = (weighted / row_sum[:, :, None]).astype(jnp.bfloat16)
    result = jnp.transpose(result, (1, 0, 2)).reshape(patch_rows, width_dev)
    attended = lax.all_to_all(result, "head", split_axis=0, concat_axis=1, tiled=True)
    return (attended, key_cache)

SPLIT = 4
MESH_TYPE = pl.DeviceIdType.MESH


def rms_rows(source, gain):
    values = source.astype(jnp.float32)
    mean_square = jnp.mean(values * values, axis=1, keepdims=True)
    return (values * lax.rsqrt(mean_square + EPSILON) * gain).astype(jnp.bfloat16)


def kernel(
    fresh_q, fresh_k, fresh_v, stale_k, stale_v, q_gain, k_gain,
    attended, key_cache,
    raw_q, raw_k, gains, own, fresh_rows, stale_rows, result,
    fresh_send, fresh_recv, stale_send, stale_recv, pass_send, pass_recv,
    out_send, out_recv, cache_send, cache_recv, local_sem,
):
    half_rows = fresh_q.shape[0]
    patch_rows, width_dev = stale_k.shape
    width = width_dev // SPLIT
    heads = width // HD
    chunk = SPLIT * patch_rows

    patch, x = lax.axis_index("patch"), lax.axis_index("head")
    core, y = lax.rem(patch, 2), lax.rem(patch // 2, 2)
    low, high = lax.rem(patch // 4, 2), patch // 8

    def flip(bit, by):
        return lax.rem(bit + by, 2)

    def patch_at(by_high, by_low, by_y, by_core=0):
        return flip(high, by_high) * 8 + flip(low, by_low) * 4 + flip(y, by_y) * 2 + flip(core, by_core)

    def group_at(by_low, by_y):
        return flip(low, by_low) * 2 + flip(y, by_y)

    def rows_of(index, size):
        return pl.ds(pl.multiple_of(index * size, size), size)

    def columns_of(index):
        return pl.ds(pl.multiple_of(index * width, width), width)

    def head_columns(dx, dl, dy, h):
        first = (flip(x, dx) * SPLIT + group_at(dl, dy)) * width + h * HD
        return pl.ds(pl.multiple_of(first, HD), HD)

    cube = [(dx, dl, dy) for dx in range(2) for dl in range(2) for dy in range(2)]
    plane = [(dh, dl, dy) for dh in range(2) for dl in range(2) for dy in range(2)]
    sibling = (patch_at(0, 0, 0, 1), x)

    barrier = pltpu.get_barrier_semaphore()
    partners = [(patch_at(0, dl, dy), flip(x, dx)) for dx, dl, dy in cube[1:]]
    partners += [(patch_at(1, dl, dy), x) for dh, dl, dy in plane[4:]]
    partners += [sibling]
    for partner in partners:
        pl.semaphore_signal(barrier, inc=1, device_id=partner, device_id_type=MESH_TYPE)

    started, local = [], []

    def send(source, target, send_sem, recv_sem, device):
        copy = pltpu.make_async_remote_copy(
            src_ref=source, dst_ref=target, send_sem=send_sem, recv_sem=recv_sem,
            device_id=device, device_id_type=MESH_TYPE,
        )
        copy.start()
        started.append(copy)

    def arrive(target, send_sem, recv_sem, device):
        pltpu.make_async_remote_copy(
            src_ref=target, dst_ref=target, send_sem=send_sem, recv_sem=recv_sem,
            device_id=device, device_id_type=MESH_TYPE,
        ).wait_recv()

    def place(source, target):
        copy = pltpu.make_async_copy(source, target, local_sem.at[len(local)])
        copy.start()
        local.append(copy)
        return copy

    place(fresh_v, own.at[2])
    place(fresh_q, raw_q)
    place(fresh_k, raw_k)
    place(q_gain, gains.at[0])
    place(k_gain, gains.at[1])
    pl.semaphore_wait(barrier, len(partners))

    my_rows = rows_of(group_at(0, 0) * 2 + x, half_rows)

    def key_rows_of(high_of, low_of, core_of, y_of):
        return rows_of(((high_of * 2 + low_of) * 2 + core_of) * 2 + y_of, patch_rows)

    def send_stale(i):
        dh, dl, dy = plane[i]
        rows = key_rows_of(high, low, core, y)
        for t, source in enumerate((stale_k, stale_v)):
            block = source.at[:, columns_of(group_at(dl, dy))]
            if i == 0:
                place(block, stale_rows.at[t, rows])
            else:
                send(
                    block, stale_rows.at[t, rows], stale_send.at[t, i], stale_recv.at[t, i],
                    (patch_at(dh, dl, dy), x),
                )

    for i in range(4, 8):
        send_stale(i)
    for copy in local[:5]:
        copy.wait()
    own[0] = rms_rows(raw_q[...], gains[0])
    own[1] = rms_rows(raw_k[...], gains[1])
    for i, (dx, dl, dy) in enumerate(cube):
        block = own.at[:, :, columns_of(flip(x, dx) * SPLIT + group_at(dl, dy))]
        if i == 0:
            place(block, fresh_rows.at[:, my_rows])
        else:
            send(
                block, fresh_rows.at[:, my_rows], fresh_send.at[i], fresh_recv.at[i],
                (patch_at(0, dl, dy), flip(x, dx)),
            )
    for i in range(4):
        send_stale(i)
    cache_rows = rows_of(x, half_rows)
    side = pl.ds(pl.multiple_of(x * width_dev, width_dev), width_dev)
    other_side = pl.ds(pl.multiple_of((1 - x) * width_dev, width_dev), width_dev)
    place(own.at[1, :, side], key_cache.at[cache_rows])
    send(
        own.at[1, :, other_side], key_cache.at[cache_rows],
        cache_send.at[0], cache_recv.at[0], (patch, 1 - x),
    )
    for copy in local[5:]:
        copy.wait()

    for i, (dx, dl, dy) in enumerate(cube):
        if i > 0:
            arrive(
                fresh_rows.at[:, rows_of(group_at(dl, dy) * 2 + flip(x, dx), half_rows)],
                fresh_send.at[i], fresh_recv.at[i], (patch_at(0, dl, dy), flip(x, dx)),
            )

    factor = HD ** (-0.5) * 1.4426950408889634
    state = [None] * heads
    row_patch = lax.broadcasted_iota(jnp.int32, (chunk, 1), 0) // patch_rows
    column_patch = lax.broadcasted_iota(jnp.int32, (1, chunk), 1) // patch_rows

    def attend(h, keys, values, masked):
        columns = slice(h * HD, (h + 1) * HD)
        scores = lax.dot_general(
            fresh_rows[0, :, columns], keys[:, columns], (((1,), (1,)), ((), ())),
            preferred_element_type=jnp.float32,
        )
        if masked is not None:
            scores = jnp.where(masked, 2.0 * LOWEST, scores)
        new_max = jnp.max(scores, axis=1, keepdims=True)
        if state[h] is not None:
            row_max, row_sum, weighted = state[h]
            new_max = jnp.maximum(row_max, new_max)
        weights = jnp.exp2((scores - new_max) * factor)
        new_sum = jnp.sum(weights, axis=1, keepdims=True)
        added = jnp.dot(
            weights.astype(jnp.bfloat16), values[:, columns], preferred_element_type=jnp.float32
        )
        if state[h] is not None:
            rescale = jnp.exp2((row_max - new_max) * factor)
            new_sum += row_sum * rescale
            added += weighted * rescale
        state[h] = (new_max, new_sum, added)

    def give_back(h):
        _, row_sum, weighted = state[h]
        columns = slice(h * HD, (h + 1) * HD)
        result[:, columns] = (weighted / row_sum).astype(jnp.bfloat16)
        for i, (dx, dl, dy) in enumerate(cube):
            block = result.at[rows_of(group_at(dl, dy) * 2 + flip(x, dx), half_rows), columns]
            target = attended.at[:, head_columns(0, 0, 0, h)]
            if i == 0:
                place(block, target)
            else:
                send(
                    block, target, out_send.at[h, i], out_recv.at[h, i],
                    (patch_at(0, dl, dy), flip(x, dx)),
                )

    for h in range(heads):
        attend(h, fresh_rows.at[1], fresh_rows.at[2], row_patch != column_patch)

    for dh, dl in ((1, 0), (1, 1), (0, 0), (0, 1)):
        for i in range(8):
            if i > 0 and plane[i][:2] == (dh, dl):
                rows = key_rows_of(flip(high, dh), flip(low, dl), core, flip(y, plane[i][2]))
                for t in range(2):
                    arrive(
                        stale_rows.at[t, rows], stale_send.at[t, i], stale_recv.at[t, i],
                        (patch_at(*plane[i]), x),
                    )
        step = dh * 2 + dl
        block = flip(high, dh) * 2 + flip(low, dl)
        rows = rows_of(block * 2 + core, 2 * patch_rows)
        send(
            stale_rows.at[:, rows], stale_rows.at[:, rows],
            pass_send.at[step], pass_recv.at[step], sibling,
        )
        rows = rows_of(block * 2 + 1 - core, 2 * patch_rows)
        arrive(stale_rows.at[:, rows], pass_send.at[step], pass_recv.at[step], sibling)
        block = rows_of(block, chunk)
        masked = None
        if dh == 0:
            row_key = jnp.where(row_patch // 2 == flip(low, dl), row_patch % 2, -1)
            column_key = jnp.where(column_patch // 2 == core, column_patch % 2, -2)
            masked = row_key == column_key
        for h in range(heads):
            attend(h, stale_rows.at[0, block], stale_rows.at[1, block], masked)
            if (dh, dl) == (0, 1):
                give_back(h)

    for copy in started:
        copy.wait_send()
    arrive(key_cache.at[rows_of(1 - x, half_rows)], cache_send.at[0], cache_recv.at[0], (patch, 1 - x))
    for h in range(heads):
        for i, (dx, dl, dy) in enumerate(cube):
            if i > 0:
                arrive(
                    attended.at[:, head_columns(dx, dl, dy, h)],
                    out_send.at[h, i], out_recv.at[h, i], (patch_at(0, dl, dy), flip(x, dx)),
                )
    for copy in local[-heads:]:
        copy.wait()


def kernel_body(fresh_q, fresh_k, fresh_v, stale_k, stale_v, q_gain, k_gain):
    half_rows, width_all = fresh_q.shape
    patch_rows, width_dev = stale_k.shape
    tokens = patch_rows * lax.axis_size("patch")
    width = width_dev // SPLIT
    group = (SPLIT * patch_rows, width)
    bf16 = jnp.bfloat16
    in_hbm = pl.BlockSpec(memory_space=pltpu.HBM)
    sems = [(8,), (8,), (2, 8), (2, 8), (4,), (4,)]
    heads = width // HD
    sems += [(heads, 8), (heads, 8), (1,), (1,), (9 + heads,)]
    pairs = (width_dev // HD) * patch_rows * tokens
    return pl.pallas_call(
        kernel,
        out_shape=[
            jax.ShapeDtypeStruct((half_rows, width_all), bf16),
            jax.ShapeDtypeStruct((patch_rows, width_dev), bf16),
        ],
        in_specs=[in_hbm] * 7,
        out_specs=[in_hbm] * 2,
        scratch_shapes=[
            pltpu.VMEM((half_rows, width_all), bf16),
            pltpu.VMEM((half_rows, width_all), bf16),
            pltpu.VMEM((2, 1, width_all), jnp.float32),
            pltpu.VMEM((3, half_rows, width_all), bf16),
            pltpu.VMEM((3,) + group, bf16),
            pltpu.VMEM((2, tokens, width), bf16),
            pltpu.VMEM(group, bf16),
        ]
        + [pltpu.SemaphoreType.DMA(shape) for shape in sems],
        compiler_params=pltpu.CompilerParams(
            collective_id=0, has_side_effects=True, vmem_limit_bytes=62 * 1024 * 1024
        ),
        cost_estimate=pl.CostEstimate(
            flops=4 * pairs * HD, bytes_accessed=8 * tokens * width, transcendentals=pairs
        ),
    )(fresh_q, fresh_k, fresh_v, stale_k, stale_v, q_gain[None, :], k_gain[None, :])


def solution(mesh):
    placed = (
        P(("patch", "head"), None),
        P(("patch", "head"), None),
        P(("patch", "head"), None),
        P("patch", "head"),
        P("patch", "head"),
        P(),
        P(),
    )
    fits = mesh.shape["patch"] == 16 and mesh.shape["head"] == 2
    return jax.shard_map(
        kernel_body if fits else body,
        mesh=mesh,
        in_specs=placed,
        out_specs=(P(("patch", "head"), None), P("patch", "head")),
        check_vma=False,
    )
```

```python
import jax
import jax.numpy as jnp
from jax import lax
from jax.experimental import pallas as pl
from jax.experimental.pallas import tpu as pltpu
from jax.sharding import PartitionSpec as P

HEADS = 24
HD = 128


EPSILON = 1e-06
LOWEST = -1e30


def scale_rows(source, square_sum, gain, width_all):
    values = source.astype(jnp.float32)
    factor = lax.rsqrt(square_sum[:, None] / width_all + EPSILON)
    return (values * factor * gain[None, :]).astype(jnp.bfloat16)


def heads_view(source, heads_dev):
    return source.reshape(source.shape[0], heads_dev, source.shape[1] // heads_dev)


def scaled_scores(queries, key_rows):
    score_scale = HD ** (-0.5)
    return (
        jnp.einsum("qhe,khe->hqk", queries, key_rows, preferred_element_type=jnp.float32)
        * score_scale
    )


def block_stats(scores, value_rows):
    row_max = jnp.max(scores, axis=2)
    weights = jnp.exp(scores - row_max[:, :, None])
    row_sum = jnp.sum(weights, axis=2)
    weighted = jnp.einsum(
        "hqk,khe->hqe", weights.astype(jnp.bfloat16), value_rows, preferred_element_type=jnp.float32
    )
    return (row_max, row_sum, weighted)


def absorb(carried, scores, value_rows):
    row_max, row_sum, weighted = carried
    new_max = jnp.maximum(row_max, jnp.max(scores, axis=2))
    rescale = jnp.exp(row_max - new_max)
    weights = jnp.exp(scores - new_max[:, :, None])
    row_sum = row_sum * rescale + jnp.sum(weights, axis=2)
    added = jnp.einsum(
        "hqk,khe->hqe", weights.astype(jnp.bfloat16), value_rows, preferred_element_type=jnp.float32
    )
    return (new_max, row_sum, weighted * rescale[:, :, None] + added)


def body(fresh_q, fresh_k, fresh_v, stale_k, stale_v, q_gain, k_gain):
    groups = lax.axis_size("head")
    heads_dev = HEADS // groups
    width_dev = heads_dev * HD
    width_all = q_gain.shape[0]
    local_q, local_k, local_v = (
        lax.all_to_all(fresh_q, "head", split_axis=1, concat_axis=0, tiled=True),
        lax.all_to_all(fresh_k, "head", split_axis=1, concat_axis=0, tiled=True),
        lax.all_to_all(fresh_v, "head", split_axis=1, concat_axis=0, tiled=True),
    )
    first_col = lax.axis_index("head") * width_dev
    gain_q = lax.dynamic_slice_in_dim(q_gain, first_col, width_dev, 0)
    gain_k = lax.dynamic_slice_in_dim(k_gain, first_col, width_dev, 0)
    squares_q = jnp.sum(jnp.square(local_q.astype(jnp.float32)), axis=1)
    squares_k = jnp.sum(jnp.square(local_k.astype(jnp.float32)), axis=1)
    total_q, total_k = lax.psum((squares_q, squares_k), "head")
    normed_q = scale_rows(local_q, total_q, gain_q, width_all)
    key_cache = scale_rows(local_k, total_k, gain_k, width_all)
    patch_rows = normed_q.shape[0]
    my_patch = lax.axis_index("patch")
    query_view = heads_view(normed_q, heads_dev)
    fresh_state = block_stats(
        scaled_scores(query_view, heads_view(key_cache, heads_dev)), heads_view(local_v, heads_dev)
    )
    segment = (
        lax.all_gather(stale_k, "patch", axis=0, tiled=True),
        lax.all_gather(stale_v, "patch", axis=0, tiled=True),
    )
    key_rows = heads_view(segment[0], heads_dev)
    value_rows = heads_view(segment[1], heads_dev)
    scores = scaled_scores(query_view, key_rows)
    owner_patch = jnp.arange(segment[0].shape[0], dtype=jnp.int32) // patch_rows
    scores = jnp.where((owner_patch == my_patch)[None, None, :], 2.0 * LOWEST, scores)
    folded = absorb(fresh_state, scores, value_rows)
    row_max, row_sum, weighted = folded
    result = (weighted / row_sum[:, :, None]).astype(jnp.bfloat16)
    result = jnp.transpose(result, (1, 0, 2)).reshape(patch_rows, width_dev)
    attended = lax.all_to_all(result, "head", split_axis=0, concat_axis=1, tiled=True)
    return (attended, key_cache)

SPLIT = 4
MESH_TYPE = pl.DeviceIdType.MESH


def rms_rows(source, gain):
    values = source.astype(jnp.float32)
    mean_square = jnp.mean(values * values, axis=1, keepdims=True)
    return (values * lax.rsqrt(mean_square + EPSILON) * gain).astype(jnp.bfloat16)


def kernel(
    fresh_q, fresh_k, fresh_v, stale_k, stale_v, q_gain, k_gain,
    attended, key_cache,
    raw_q, raw_k, gains, own, fresh_rows, stale_rows, result,
    fresh_send, fresh_recv, stale_send, stale_recv, pass_send, pass_recv,
    out_send, out_recv, cache_send, cache_recv, local_sem,
):
    half_rows = fresh_q.shape[0]
    patch_rows, width_dev = stale_k.shape
    width = width_dev // SPLIT
    heads = width // HD
    chunk = SPLIT * patch_rows

    patch, x = lax.axis_index("patch"), lax.axis_index("head")
    core, y = lax.rem(patch, 2), lax.rem(patch // 2, 2)
    low, high = lax.rem(patch // 4, 2), patch // 8

    def flip(bit, by):
        return lax.rem(bit + by, 2)

    def patch_at(by_high, by_low, by_y, by_core=0):
        return flip(high, by_high) * 8 + flip(low, by_low) * 4 + flip(y, by_y) * 2 + flip(core, by_core)

    def group_at(by_low, by_y):
        return flip(low, by_low) * 2 + flip(y, by_y)

    def rows_of(index, size):
        return pl.ds(pl.multiple_of(index * size, size), size)

    def columns_of(index):
        return pl.ds(pl.multiple_of(index * width, width), width)

    def head_columns(dx, dl, dy, h):
        first = (flip(x, dx) * SPLIT + group_at(dl, dy)) * width + h * HD
        return pl.ds(pl.multiple_of(first, HD), HD)

    cube = [(dx, dl, dy) for dx in range(2) for dl in range(2) for dy in range(2)]
    plane = [(dh, dl, dy) for dh in range(2) for dl in range(2) for dy in range(2)]
    sibling = (patch_at(0, 0, 0, 1), x)

    barrier = pltpu.get_barrier_semaphore()
    partners = [(patch_at(0, dl, dy), flip(x, dx)) for dx, dl, dy in cube[1:]]
    partners += [(patch_at(1, dl, dy), x) for dh, dl, dy in plane[4:]]
    partners += [sibling]
    for partner in partners:
        pl.semaphore_signal(barrier, inc=1, device_id=partner, device_id_type=MESH_TYPE)

    started, local = [], []

    def send(source, target, send_sem, recv_sem, device):
        copy = pltpu.make_async_remote_copy(
            src_ref=source, dst_ref=target, send_sem=send_sem, recv_sem=recv_sem,
            device_id=device, device_id_type=MESH_TYPE,
        )
        copy.start()
        started.append(copy)

    def arrive(target, send_sem, recv_sem, device):
        pltpu.make_async_remote_copy(
            src_ref=target, dst_ref=target, send_sem=send_sem, recv_sem=recv_sem,
            device_id=device, device_id_type=MESH_TYPE,
        ).wait_recv()

    def place(source, target):
        copy = pltpu.make_async_copy(source, target, local_sem.at[len(local)])
        copy.start()
        local.append(copy)
        return copy

    place(fresh_v, own.at[2])
    place(fresh_q, raw_q)
    place(fresh_k, raw_k)
    place(q_gain, gains.at[0])
    place(k_gain, gains.at[1])
    pl.semaphore_wait(barrier, len(partners))

    my_rows = rows_of(group_at(0, 0) * 2 + x, half_rows)

    def key_rows_of(high_of, low_of, core_of, y_of):
        return rows_of(((high_of * 2 + low_of) * 2 + core_of) * 2 + y_of, patch_rows)

    def send_stale(i):
        dh, dl, dy = plane[i]
        rows = key_rows_of(high, low, core, y)
        for t, source in enumerate((stale_k, stale_v)):
            block = source.at[:, columns_of(group_at(dl, dy))]
            if i == 0:
                place(block, stale_rows.at[t, rows])
            else:
                send(
                    block, stale_rows.at[t, rows], stale_send.at[t, i], stale_recv.at[t, i],
                    (patch_at(dh, dl, dy), x),
                )

    def send_fresh(i):
        dx, dl, dy = cube[i]
        block = own.at[:, :, columns_of(flip(x, dx) * SPLIT + group_at(dl, dy))]
        if i == 0:
            place(block, fresh_rows.at[:, my_rows])
        else:
            send(
                block, fresh_rows.at[:, my_rows], fresh_send.at[i], fresh_recv.at[i],
                (patch_at(0, dl, dy), flip(x, dx)),
            )

    for i in (4, 2, 5, 3, 1, 0):
        send_stale(i)
    for copy in local[:5]:
        copy.wait()
    own[0] = rms_rows(raw_q[...], gains[0])
    own[1] = rms_rows(raw_k[...], gains[1])
    send_fresh(2)
    send_fresh(3)
    send_stale(6)
    send_fresh(6)
    send_fresh(7)
    send_stale(7)
    for i in (1, 4, 5, 0):
        send_fresh(i)
    cache_rows = rows_of(x, half_rows)
    side = pl.ds(pl.multiple_of(x * width_dev, width_dev), width_dev)
    other_side = pl.ds(pl.multiple_of((1 - x) * width_dev, width_dev), width_dev)
    place(own.at[1, :, side], key_cache.at[cache_rows])
    send(
        own.at[1, :, other_side], key_cache.at[cache_rows],
        cache_send.at[0], cache_recv.at[0], (patch, 1 - x),
    )
    for copy in local[5:]:
        copy.wait()

    for i, (dx, dl, dy) in enumerate(cube):
        if i > 0:
            arrive(
                fresh_rows.at[:, rows_of(group_at(dl, dy) * 2 + flip(x, dx), half_rows)],
                fresh_send.at[i], fresh_recv.at[i], (patch_at(0, dl, dy), flip(x, dx)),
            )

    factor = HD ** (-0.5) * 1.4426950408889634
    state = [None] * heads
    row_patch = lax.broadcasted_iota(jnp.int32, (chunk, 1), 0) // patch_rows
    column_patch = lax.broadcasted_iota(jnp.int32, (1, chunk), 1) // patch_rows

    def attend(h, keys, values, masked):
        columns = slice(h * HD, (h + 1) * HD)
        scores = lax.dot_general(
            fresh_rows[0, :, columns], keys[:, columns], (((1,), (1,)), ((), ())),
            preferred_element_type=jnp.float32,
        )
        if masked is not None:
            scores = jnp.where(masked, 2.0 * LOWEST, scores)
        new_max = jnp.max(scores, axis=1, keepdims=True)
        if state[h] is not None:
            row_max, row_sum, weighted = state[h]
            new_max = jnp.maximum(row_max, new_max)
        weights = jnp.exp2((scores - new_max) * factor)
        new_sum = jnp.sum(weights, axis=1, keepdims=True)
        added = jnp.dot(
            weights.astype(jnp.bfloat16), values[:, columns], preferred_element_type=jnp.float32
        )
        if state[h] is not None:
            rescale = jnp.exp2((row_max - new_max) * factor)
            new_sum += row_sum * rescale
            added += weighted * rescale
        state[h] = (new_max, new_sum, added)

    def give_back(h):
        _, row_sum, weighted = state[h]
        columns = slice(h * HD, (h + 1) * HD)
        result[:, columns] = (weighted / row_sum).astype(jnp.bfloat16)
        for i, (dx, dl, dy) in enumerate(cube):
            block = result.at[rows_of(group_at(dl, dy) * 2 + flip(x, dx), half_rows), columns]
            target = attended.at[:, head_columns(0, 0, 0, h)]
            if i == 0:
                place(block, target)
            else:
                send(
                    block, target, out_send.at[h, i], out_recv.at[h, i],
                    (patch_at(0, dl, dy), flip(x, dx)),
                )

    for h in range(heads):
        attend(h, fresh_rows.at[1], fresh_rows.at[2], row_patch != column_patch)

    for dh, dl in ((0, 0), (0, 1), (1, 0), (1, 1)):
        for i in range(8):
            if i > 0 and plane[i][:2] == (dh, dl):
                rows = key_rows_of(flip(high, dh), flip(low, dl), core, flip(y, plane[i][2]))
                for t in range(2):
                    arrive(
                        stale_rows.at[t, rows], stale_send.at[t, i], stale_recv.at[t, i],
                        (patch_at(*plane[i]), x),
                    )
        step = dh * 2 + dl
        block = flip(high, dh) * 2 + flip(low, dl)
        rows = rows_of(block * 2 + core, 2 * patch_rows)
        send(
            stale_rows.at[:, rows], stale_rows.at[:, rows],
            pass_send.at[step], pass_recv.at[step], sibling,
        )
        rows = rows_of(block * 2 + 1 - core, 2 * patch_rows)
        arrive(stale_rows.at[:, rows], pass_send.at[step], pass_recv.at[step], sibling)
        block = rows_of(block, chunk)
        masked = None
        if dh == 0:
            row_key = jnp.where(row_patch // 2 == flip(low, dl), row_patch % 2, -1)
            column_key = jnp.where(column_patch // 2 == core, column_patch % 2, -2)
            masked = row_key == column_key
        for h in range(heads):
            attend(h, stale_rows.at[0, block], stale_rows.at[1, block], masked)
            if (dh, dl) == (1, 1):
                give_back(h)

    for copy in started:
        copy.wait_send()
    arrive(key_cache.at[rows_of(1 - x, half_rows)], cache_send.at[0], cache_recv.at[0], (patch, 1 - x))
    for h in range(heads):
        for i, (dx, dl, dy) in enumerate(cube):
            if i > 0:
                arrive(
                    attended.at[:, head_columns(dx, dl, dy, h)],
                    out_send.at[h, i], out_recv.at[h, i], (patch_at(0, dl, dy), flip(x, dx)),
                )
    for copy in local[-heads:]:
        copy.wait()


def kernel_body(fresh_q, fresh_k, fresh_v, stale_k, stale_v, q_gain, k_gain):
    half_rows, width_all = fresh_q.shape
    patch_rows, width_dev = stale_k.shape
    tokens = patch_rows * lax.axis_size("patch")
    width = width_dev // SPLIT
    group = (SPLIT * patch_rows, width)
    bf16 = jnp.bfloat16
    in_hbm = pl.BlockSpec(memory_space=pltpu.HBM)
    sems = [(8,), (8,), (2, 8), (2, 8), (4,), (4,)]
    heads = width // HD
    sems += [(heads, 8), (heads, 8), (1,), (1,), (9 + heads,)]
    pairs = (width_dev // HD) * patch_rows * tokens
    return pl.pallas_call(
        kernel,
        out_shape=[
            jax.ShapeDtypeStruct((half_rows, width_all), bf16),
            jax.ShapeDtypeStruct((patch_rows, width_dev), bf16),
        ],
        in_specs=[in_hbm] * 7,
        out_specs=[in_hbm] * 2,
        scratch_shapes=[
            pltpu.VMEM((half_rows, width_all), bf16),
            pltpu.VMEM((half_rows, width_all), bf16),
            pltpu.VMEM((2, 1, width_all), jnp.float32),
            pltpu.VMEM((3, half_rows, width_all), bf16),
            pltpu.VMEM((3,) + group, bf16),
            pltpu.VMEM((2, tokens, width), bf16),
            pltpu.VMEM(group, bf16),
        ]
        + [pltpu.SemaphoreType.DMA(shape) for shape in sems],
        compiler_params=pltpu.CompilerParams(
            collective_id=0, has_side_effects=True, vmem_limit_bytes=62 * 1024 * 1024
        ),
        cost_estimate=pl.CostEstimate(
            flops=4 * pairs * HD, bytes_accessed=8 * tokens * width, transcendentals=pairs
        ),
    )(fresh_q, fresh_k, fresh_v, stale_k, stale_v, q_gain[None, :], k_gain[None, :])


def solution(mesh):
    placed = (
        P(("patch", "head"), None),
        P(("patch", "head"), None),
        P(("patch", "head"), None),
        P("patch", "head"),
        P("patch", "head"),
        P(),
        P(),
    )
    fits = mesh.shape["patch"] == 16 and mesh.shape["head"] == 2
    return jax.shard_map(
        kernel_body if fits else body,
        mesh=mesh,
        in_specs=placed,
        out_specs=(P(("patch", "head"), None), P("patch", "head")),
        check_vma=False,
    )
```

```python
import jax
import jax.numpy as jnp
from jax import lax
from jax.experimental import pallas as pl
from jax.experimental.pallas import tpu as pltpu
from jax.sharding import PartitionSpec as P

HEADS = 24
HD = 128


EPSILON = 1e-06
LOWEST = -1e30


def scale_rows(source, square_sum, gain, width_all):
    values = source.astype(jnp.float32)
    factor = lax.rsqrt(square_sum[:, None] / width_all + EPSILON)
    return (values * factor * gain[None, :]).astype(jnp.bfloat16)


def heads_view(source, heads_dev):
    return source.reshape(source.shape[0], heads_dev, source.shape[1] // heads_dev)


def scaled_scores(queries, key_rows):
    score_scale = HD ** (-0.5)
    return (
        jnp.einsum("qhe,khe->hqk", queries, key_rows, preferred_element_type=jnp.float32)
        * score_scale
    )


def block_stats(scores, value_rows):
    row_max = jnp.max(scores, axis=2)
    weights = jnp.exp(scores - row_max[:, :, None])
    row_sum = jnp.sum(weights, axis=2)
    weighted = jnp.einsum(
        "hqk,khe->hqe", weights.astype(jnp.bfloat16), value_rows, preferred_element_type=jnp.float32
    )
    return (row_max, row_sum, weighted)


def absorb(carried, scores, value_rows):
    row_max, row_sum, weighted = carried
    new_max = jnp.maximum(row_max, jnp.max(scores, axis=2))
    rescale = jnp.exp(row_max - new_max)
    weights = jnp.exp(scores - new_max[:, :, None])
    row_sum = row_sum * rescale + jnp.sum(weights, axis=2)
    added = jnp.einsum(
        "hqk,khe->hqe", weights.astype(jnp.bfloat16), value_rows, preferred_element_type=jnp.float32
    )
    return (new_max, row_sum, weighted * rescale[:, :, None] + added)


def body(fresh_q, fresh_k, fresh_v, stale_k, stale_v, q_gain, k_gain):
    groups = lax.axis_size("head")
    heads_dev = HEADS // groups
    width_dev = heads_dev * HD
    width_all = q_gain.shape[0]
    local_q, local_k, local_v = (
        lax.all_to_all(fresh_q, "head", split_axis=1, concat_axis=0, tiled=True),
        lax.all_to_all(fresh_k, "head", split_axis=1, concat_axis=0, tiled=True),
        lax.all_to_all(fresh_v, "head", split_axis=1, concat_axis=0, tiled=True),
    )
    first_col = lax.axis_index("head") * width_dev
    gain_q = lax.dynamic_slice_in_dim(q_gain, first_col, width_dev, 0)
    gain_k = lax.dynamic_slice_in_dim(k_gain, first_col, width_dev, 0)
    squares_q = jnp.sum(jnp.square(local_q.astype(jnp.float32)), axis=1)
    squares_k = jnp.sum(jnp.square(local_k.astype(jnp.float32)), axis=1)
    total_q, total_k = lax.psum((squares_q, squares_k), "head")
    normed_q = scale_rows(local_q, total_q, gain_q, width_all)
    key_cache = scale_rows(local_k, total_k, gain_k, width_all)
    patch_rows = normed_q.shape[0]
    my_patch = lax.axis_index("patch")
    query_view = heads_view(normed_q, heads_dev)
    fresh_state = block_stats(
        scaled_scores(query_view, heads_view(key_cache, heads_dev)), heads_view(local_v, heads_dev)
    )
    segment = (
        lax.all_gather(stale_k, "patch", axis=0, tiled=True),
        lax.all_gather(stale_v, "patch", axis=0, tiled=True),
    )
    key_rows = heads_view(segment[0], heads_dev)
    value_rows = heads_view(segment[1], heads_dev)
    scores = scaled_scores(query_view, key_rows)
    owner_patch = jnp.arange(segment[0].shape[0], dtype=jnp.int32) // patch_rows
    scores = jnp.where((owner_patch == my_patch)[None, None, :], 2.0 * LOWEST, scores)
    folded = absorb(fresh_state, scores, value_rows)
    row_max, row_sum, weighted = folded
    result = (weighted / row_sum[:, :, None]).astype(jnp.bfloat16)
    result = jnp.transpose(result, (1, 0, 2)).reshape(patch_rows, width_dev)
    attended = lax.all_to_all(result, "head", split_axis=0, concat_axis=1, tiled=True)
    return (attended, key_cache)

SPLIT = 4
MESH_TYPE = pl.DeviceIdType.MESH


def rms_rows(source, gain):
    values = source.astype(jnp.float32)
    mean_square = jnp.mean(values * values, axis=1, keepdims=True)
    return (values * lax.rsqrt(mean_square + EPSILON) * gain).astype(jnp.bfloat16)


def kernel(
    fresh_q, fresh_k, fresh_v, stale_k, stale_v, q_gain, k_gain,
    attended, key_cache,
    raw_q, raw_k, gains, own, fresh_rows, stale_rows, result,
    fresh_send, fresh_recv, stale_send, stale_recv, pass_send, pass_recv,
    out_send, out_recv, cache_send, cache_recv, local_sem,
):
    half_rows = fresh_q.shape[0]
    patch_rows, width_dev = stale_k.shape
    width = width_dev // SPLIT
    heads = width // HD
    chunk = SPLIT * patch_rows

    patch, x = lax.axis_index("patch"), lax.axis_index("head")
    core, y = lax.rem(patch, 2), lax.rem(patch // 2, 2)
    low, high = lax.rem(patch // 4, 2), patch // 8

    def flip(bit, by):
        return lax.rem(bit + by, 2)

    def patch_at(by_high, by_low, by_y, by_core=0):
        return flip(high, by_high) * 8 + flip(low, by_low) * 4 + flip(y, by_y) * 2 + flip(core, by_core)

    def group_at(by_low, by_y):
        return flip(low, by_low) * 2 + flip(y, by_y)

    def rows_of(index, size):
        return pl.ds(pl.multiple_of(index * size, size), size)

    def columns_of(index):
        return pl.ds(pl.multiple_of(index * width, width), width)

    def head_columns(dx, dl, dy, h):
        first = (flip(x, dx) * SPLIT + group_at(dl, dy)) * width + h * HD
        return pl.ds(pl.multiple_of(first, HD), HD)

    cube = [(dx, dl, dy) for dx in range(2) for dl in range(2) for dy in range(2)]
    plane = [(dh, dl, dy) for dh in range(2) for dl in range(2) for dy in range(2)]
    sibling = (patch_at(0, 0, 0, 1), x)

    barrier = pltpu.get_barrier_semaphore()
    partners = [(patch_at(0, dl, dy), flip(x, dx)) for dx, dl, dy in cube[1:]]
    partners += [(patch_at(1, dl, dy), x) for dh, dl, dy in plane[4:]]
    partners += [sibling]
    for partner in partners:
        pl.semaphore_signal(barrier, inc=1, device_id=partner, device_id_type=MESH_TYPE)

    started, local = [], []

    def send(source, target, send_sem, recv_sem, device, now=True):
        copy = pltpu.make_async_remote_copy(
            src_ref=source, dst_ref=target, send_sem=send_sem, recv_sem=recv_sem,
            device_id=device, device_id_type=MESH_TYPE,
        )
        if now:
            copy.start()
        started.append(copy)

    def arrive(target, send_sem, recv_sem, device):
        pltpu.make_async_remote_copy(
            src_ref=target, dst_ref=target, send_sem=send_sem, recv_sem=recv_sem,
            device_id=device, device_id_type=MESH_TYPE,
        ).wait_recv()

    def place(source, target):
        copy = pltpu.make_async_copy(source, target, local_sem.at[len(local)])
        copy.start()
        local.append(copy)
        return copy

    place(fresh_v, own.at[2])
    place(fresh_q, raw_q)
    place(fresh_k, raw_k)
    place(q_gain, gains.at[0])
    place(k_gain, gains.at[1])
    pl.semaphore_wait(barrier, len(partners))

    my_rows = rows_of(group_at(0, 0) * 2 + x, half_rows)

    def key_rows_of(high_of, low_of, core_of, y_of):
        return rows_of(((high_of * 2 + low_of) * 2 + core_of) * 2 + y_of, patch_rows)

    def send_stale(i):
        dh, dl, dy = plane[i]
        rows = key_rows_of(high, low, core, y)
        for t, source in enumerate((stale_k, stale_v)):
            block = source.at[:, columns_of(group_at(dl, dy))]
            if i == 0:
                place(block, stale_rows.at[t, rows])
            else:
                send(
                    block, stale_rows.at[t, rows], stale_send.at[t, i], stale_recv.at[t, i],
                    (patch_at(dh, dl, dy), x), now=dh == 0,
                )

    for i in range(4, 8):
        send_stale(i)
    far = list(started)

    @pl.when(low != high)
    def _():
        for copy in far:
            copy.start()

    for copy in local[:5]:
        copy.wait()
    own[0] = rms_rows(raw_q[...], gains[0])
    own[1] = rms_rows(raw_k[...], gains[1])
    for i, (dx, dl, dy) in enumerate(cube):
        block = own.at[:, :, columns_of(flip(x, dx) * SPLIT + group_at(dl, dy))]
        if i == 0:
            place(block, fresh_rows.at[:, my_rows])
        else:
            send(
                block, fresh_rows.at[:, my_rows], fresh_send.at[i], fresh_recv.at[i],
                (patch_at(0, dl, dy), flip(x, dx)),
            )
    for i in range(4):
        send_stale(i)

    @pl.when(low == high)
    def _():
        for copy in far:
            copy.start()

    cache_rows = rows_of(x, half_rows)
    side = pl.ds(pl.multiple_of(x * width_dev, width_dev), width_dev)
    other_side = pl.ds(pl.multiple_of((1 - x) * width_dev, width_dev), width_dev)
    place(own.at[1, :, side], key_cache.at[cache_rows])
    send(
        own.at[1, :, other_side], key_cache.at[cache_rows],
        cache_send.at[0], cache_recv.at[0], (patch, 1 - x),
    )
    for copy in local[5:]:
        copy.wait()

    for i, (dx, dl, dy) in enumerate(cube):
        if i > 0:
            arrive(
                fresh_rows.at[:, rows_of(group_at(dl, dy) * 2 + flip(x, dx), half_rows)],
                fresh_send.at[i], fresh_recv.at[i], (patch_at(0, dl, dy), flip(x, dx)),
            )

    factor = HD ** (-0.5) * 1.4426950408889634
    state = [None] * heads
    row_patch = lax.broadcasted_iota(jnp.int32, (chunk, 1), 0) // patch_rows
    column_patch = lax.broadcasted_iota(jnp.int32, (1, chunk), 1) // patch_rows

    def attend(h, keys, values, masked):
        columns = slice(h * HD, (h + 1) * HD)
        scores = lax.dot_general(
            fresh_rows[0, :, columns], keys[:, columns], (((1,), (1,)), ((), ())),
            preferred_element_type=jnp.float32,
        )
        if masked is not None:
            scores = jnp.where(masked, 2.0 * LOWEST, scores)
        new_max = jnp.max(scores, axis=1, keepdims=True)
        if state[h] is not None:
            row_max, row_sum, weighted = state[h]
            new_max = jnp.maximum(row_max, new_max)
        weights = jnp.exp2((scores - new_max) * factor)
        new_sum = jnp.sum(weights, axis=1, keepdims=True)
        added = jnp.dot(
            weights.astype(jnp.bfloat16), values[:, columns], preferred_element_type=jnp.float32
        )
        if state[h] is not None:
            rescale = jnp.exp2((row_max - new_max) * factor)
            new_sum += row_sum * rescale
            added += weighted * rescale
        state[h] = (new_max, new_sum, added)

    def give_back(h):
        _, row_sum, weighted = state[h]
        columns = slice(h * HD, (h + 1) * HD)
        result[:, columns] = (weighted / row_sum).astype(jnp.bfloat16)
        for i, (dx, dl, dy) in enumerate(cube):
            block = result.at[rows_of(group_at(dl, dy) * 2 + flip(x, dx), half_rows), columns]
            target = attended.at[:, head_columns(0, 0, 0, h)]
            if i == 0:
                place(block, target)
            else:
                send(
                    block, target, out_send.at[h, i], out_recv.at[h, i],
                    (patch_at(0, dl, dy), flip(x, dx)),
                )

    for h in range(heads):
        attend(h, fresh_rows.at[1], fresh_rows.at[2], row_patch != column_patch)

    for dh, dl in ((0, 0), (0, 1), (1, 0), (1, 1)):
        for i in range(8):
            if i > 0 and plane[i][:2] == (dh, dl):
                rows = key_rows_of(flip(high, dh), flip(low, dl), core, flip(y, plane[i][2]))
                for t in range(2):
                    arrive(
                        stale_rows.at[t, rows], stale_send.at[t, i], stale_recv.at[t, i],
                        (patch_at(*plane[i]), x),
                    )
        step = dh * 2 + dl
        block = flip(high, dh) * 2 + flip(low, dl)
        rows = rows_of(block * 2 + core, 2 * patch_rows)
        send(
            stale_rows.at[:, rows], stale_rows.at[:, rows],
            pass_send.at[step], pass_recv.at[step], sibling,
        )
        rows = rows_of(block * 2 + 1 - core, 2 * patch_rows)
        arrive(stale_rows.at[:, rows], pass_send.at[step], pass_recv.at[step], sibling)
        block = rows_of(block, chunk)
        masked = None
        if dh == 0:
            row_key = jnp.where(row_patch // 2 == flip(low, dl), row_patch % 2, -1)
            column_key = jnp.where(column_patch // 2 == core, column_patch % 2, -2)
            masked = row_key == column_key
        for h in range(heads):
            attend(h, stale_rows.at[0, block], stale_rows.at[1, block], masked)
            if (dh, dl) == (1, 1):
                give_back(h)

    for copy in started:
        copy.wait_send()
    arrive(key_cache.at[rows_of(1 - x, half_rows)], cache_send.at[0], cache_recv.at[0], (patch, 1 - x))
    for h in range(heads):
        for i, (dx, dl, dy) in enumerate(cube):
            if i > 0:
                arrive(
                    attended.at[:, head_columns(dx, dl, dy, h)],
                    out_send.at[h, i], out_recv.at[h, i], (patch_at(0, dl, dy), flip(x, dx)),
                )
    for copy in local[-heads:]:
        copy.wait()


def kernel_body(fresh_q, fresh_k, fresh_v, stale_k, stale_v, q_gain, k_gain):
    half_rows, width_all = fresh_q.shape
    patch_rows, width_dev = stale_k.shape
    tokens = patch_rows * lax.axis_size("patch")
    width = width_dev // SPLIT
    group = (SPLIT * patch_rows, width)
    bf16 = jnp.bfloat16
    in_hbm = pl.BlockSpec(memory_space=pltpu.HBM)
    sems = [(8,), (8,), (2, 8), (2, 8), (4,), (4,)]
    heads = width // HD
    sems += [(heads, 8), (heads, 8), (1,), (1,), (9 + heads,)]
    pairs = (width_dev // HD) * patch_rows * tokens
    return pl.pallas_call(
        kernel,
        out_shape=[
            jax.ShapeDtypeStruct((half_rows, width_all), bf16),
            jax.ShapeDtypeStruct((patch_rows, width_dev), bf16),
        ],
        in_specs=[in_hbm] * 7,
        out_specs=[in_hbm] * 2,
        scratch_shapes=[
            pltpu.VMEM((half_rows, width_all), bf16),
            pltpu.VMEM((half_rows, width_all), bf16),
            pltpu.VMEM((2, 1, width_all), jnp.float32),
            pltpu.VMEM((3, half_rows, width_all), bf16),
            pltpu.VMEM((3,) + group, bf16),
            pltpu.VMEM((2, tokens, width), bf16),
            pltpu.VMEM(group, bf16),
        ]
        + [pltpu.SemaphoreType.DMA(shape) for shape in sems],
        compiler_params=pltpu.CompilerParams(
            collective_id=0, has_side_effects=True, vmem_limit_bytes=62 * 1024 * 1024
        ),
        cost_estimate=pl.CostEstimate(
            flops=4 * pairs * HD, bytes_accessed=8 * tokens * width, transcendentals=pairs
        ),
    )(fresh_q, fresh_k, fresh_v, stale_k, stale_v, q_gain[None, :], k_gain[None, :])


def solution(mesh):
    placed = (
        P(("patch", "head"), None),
        P(("patch", "head"), None),
        P(("patch", "head"), None),
        P("patch", "head"),
        P("patch", "head"),
        P(),
        P(),
    )
    fits = mesh.shape["patch"] == 16 and mesh.shape["head"] == 2
    return jax.shard_map(
        kernel_body if fits else body,
        mesh=mesh,
        in_specs=placed,
        out_specs=(P(("patch", "head"), None), P("patch", "head")),
        check_vma=False,
    )
```

```python
import jax
import jax.numpy as jnp
from jax import lax
from jax.experimental import pallas as pl
from jax.experimental.pallas import tpu as pltpu
from jax.sharding import PartitionSpec as P

HEADS = 24
HD = 128


EPSILON = 1e-06
LOWEST = -1e30


def scale_rows(source, square_sum, gain, width_all):
    values = source.astype(jnp.float32)
    factor = lax.rsqrt(square_sum[:, None] / width_all + EPSILON)
    return (values * factor * gain[None, :]).astype(jnp.bfloat16)


def heads_view(source, heads_dev):
    return source.reshape(source.shape[0], heads_dev, source.shape[1] // heads_dev)


def scaled_scores(queries, key_rows):
    score_scale = HD ** (-0.5)
    return (
        jnp.einsum("qhe,khe->hqk", queries, key_rows, preferred_element_type=jnp.float32)
        * score_scale
    )


def block_stats(scores, value_rows):
    row_max = jnp.max(scores, axis=2)
    weights = jnp.exp(scores - row_max[:, :, None])
    row_sum = jnp.sum(weights, axis=2)
    weighted = jnp.einsum(
        "hqk,khe->hqe", weights.astype(jnp.bfloat16), value_rows, preferred_element_type=jnp.float32
    )
    return (row_max, row_sum, weighted)


def absorb(carried, scores, value_rows):
    row_max, row_sum, weighted = carried
    new_max = jnp.maximum(row_max, jnp.max(scores, axis=2))
    rescale = jnp.exp(row_max - new_max)
    weights = jnp.exp(scores - new_max[:, :, None])
    row_sum = row_sum * rescale + jnp.sum(weights, axis=2)
    added = jnp.einsum(
        "hqk,khe->hqe", weights.astype(jnp.bfloat16), value_rows, preferred_element_type=jnp.float32
    )
    return (new_max, row_sum, weighted * rescale[:, :, None] + added)


def body(fresh_q, fresh_k, fresh_v, stale_k, stale_v, q_gain, k_gain):
    groups = lax.axis_size("head")
    heads_dev = HEADS // groups
    width_dev = heads_dev * HD
    width_all = q_gain.shape[0]
    local_q, local_k, local_v = (
        lax.all_to_all(fresh_q, "head", split_axis=1, concat_axis=0, tiled=True),
        lax.all_to_all(fresh_k, "head", split_axis=1, concat_axis=0, tiled=True),
        lax.all_to_all(fresh_v, "head", split_axis=1, concat_axis=0, tiled=True),
    )
    first_col = lax.axis_index("head") * width_dev
    gain_q = lax.dynamic_slice_in_dim(q_gain, first_col, width_dev, 0)
    gain_k = lax.dynamic_slice_in_dim(k_gain, first_col, width_dev, 0)
    squares_q = jnp.sum(jnp.square(local_q.astype(jnp.float32)), axis=1)
    squares_k = jnp.sum(jnp.square(local_k.astype(jnp.float32)), axis=1)
    total_q, total_k = lax.psum((squares_q, squares_k), "head")
    normed_q = scale_rows(local_q, total_q, gain_q, width_all)
    key_cache = scale_rows(local_k, total_k, gain_k, width_all)
    patch_rows = normed_q.shape[0]
    my_patch = lax.axis_index("patch")
    query_view = heads_view(normed_q, heads_dev)
    fresh_state = block_stats(
        scaled_scores(query_view, heads_view(key_cache, heads_dev)), heads_view(local_v, heads_dev)
    )
    segment = (
        lax.all_gather(stale_k, "patch", axis=0, tiled=True),
        lax.all_gather(stale_v, "patch", axis=0, tiled=True),
    )
    key_rows = heads_view(segment[0], heads_dev)
    value_rows = heads_view(segment[1], heads_dev)
    scores = scaled_scores(query_view, key_rows)
    owner_patch = jnp.arange(segment[0].shape[0], dtype=jnp.int32) // patch_rows
    scores = jnp.where((owner_patch == my_patch)[None, None, :], 2.0 * LOWEST, scores)
    folded = absorb(fresh_state, scores, value_rows)
    row_max, row_sum, weighted = folded
    result = (weighted / row_sum[:, :, None]).astype(jnp.bfloat16)
    result = jnp.transpose(result, (1, 0, 2)).reshape(patch_rows, width_dev)
    attended = lax.all_to_all(result, "head", split_axis=0, concat_axis=1, tiled=True)
    return (attended, key_cache)

SPLIT = 4
MESH_TYPE = pl.DeviceIdType.MESH


def rms_rows(source, gain):
    values = source.astype(jnp.float32)
    mean_square = jnp.mean(values * values, axis=1, keepdims=True)
    return (values * lax.rsqrt(mean_square + EPSILON) * gain).astype(jnp.bfloat16)


def kernel(
    fresh_q, fresh_k, fresh_v, stale_k, stale_v, q_gain, k_gain,
    attended, key_cache,
    raw_q, raw_k, gains, own, fresh_rows, stale_rows, result,
    fresh_send, fresh_recv, stale_send, stale_recv, pass_send, pass_recv,
    out_send, out_recv, cache_send, cache_recv, local_sem,
):
    half_rows = fresh_q.shape[0]
    patch_rows, width_dev = stale_k.shape
    width = width_dev // SPLIT
    heads = width // HD
    chunk = SPLIT * patch_rows

    patch, x = lax.axis_index("patch"), lax.axis_index("head")
    core, y = lax.rem(patch, 2), lax.rem(patch // 2, 2)
    low, high = lax.rem(patch // 4, 2), patch // 8

    def flip(bit, by):
        return lax.rem(bit + by, 2)

    def patch_at(by_high, by_low, by_y, by_core=0):
        return flip(high, by_high) * 8 + flip(low, by_low) * 4 + flip(y, by_y) * 2 + flip(core, by_core)

    def group_at(by_low, by_y):
        return flip(low, by_low) * 2 + flip(y, by_y)

    def rows_of(index, size):
        return pl.ds(pl.multiple_of(index * size, size), size)

    def columns_of(index):
        return pl.ds(pl.multiple_of(index * width, width), width)

    def head_columns(dx, dl, dy, h):
        first = (flip(x, dx) * SPLIT + group_at(dl, dy)) * width + h * HD
        return pl.ds(pl.multiple_of(first, HD), HD)

    cube = [(dx, dl, dy) for dx in range(2) for dl in range(2) for dy in range(2)]
    plane = [(dh, dl, dy) for dh in range(2) for dl in range(2) for dy in range(2)]
    sibling = (patch_at(0, 0, 0, 1), x)

    barrier = pltpu.get_barrier_semaphore()
    partners = [(patch_at(0, dl, dy), flip(x, dx)) for dx, dl, dy in cube[1:]]
    partners += [(patch_at(1, dl, dy), x) for dh, dl, dy in plane[4:]]
    partners += [sibling]
    for partner in partners:
        pl.semaphore_signal(barrier, inc=1, device_id=partner, device_id_type=MESH_TYPE)

    started, local = [], []

    def send(source, target, send_sem, recv_sem, device, now=True):
        copy = pltpu.make_async_remote_copy(
            src_ref=source, dst_ref=target, send_sem=send_sem, recv_sem=recv_sem,
            device_id=device, device_id_type=MESH_TYPE,
        )
        if now:
            copy.start()
        started.append(copy)

    def arrive(target, send_sem, recv_sem, device):
        pltpu.make_async_remote_copy(
            src_ref=target, dst_ref=target, send_sem=send_sem, recv_sem=recv_sem,
            device_id=device, device_id_type=MESH_TYPE,
        ).wait_recv()

    def place(source, target):
        copy = pltpu.make_async_copy(source, target, local_sem.at[len(local)])
        copy.start()
        local.append(copy)
        return copy

    place(fresh_v, own.at[2])
    place(fresh_q, raw_q)
    place(fresh_k, raw_k)
    place(q_gain, gains.at[0])
    place(k_gain, gains.at[1])
    pl.semaphore_wait(barrier, len(partners))

    my_rows = rows_of(group_at(0, 0) * 2 + x, half_rows)

    def key_rows_of(high_of, low_of, core_of, y_of):
        return rows_of(((high_of * 2 + low_of) * 2 + core_of) * 2 + y_of, patch_rows)

    def send_stale(i):
        dh, dl, dy = plane[i]
        rows = key_rows_of(high, low, core, y)
        for t, source in enumerate((stale_k, stale_v)):
            block = source.at[:, columns_of(group_at(dl, dy))]
            if i == 0:
                place(block, stale_rows.at[t, rows])
            else:
                send(
                    block, stale_rows.at[t, rows], stale_send.at[t, i], stale_recv.at[t, i],
                    (patch_at(dh, dl, dy), x), now=dh == 0,
                )

    for i in range(4, 8):
        send_stale(i)
    far = list(started)

    @pl.when(low != high)
    def _():
        for copy in far:
            copy.start()

    for i in range(4):
        send_stale(i)
    for copy in local[:5]:
        copy.wait()
    own[0] = rms_rows(raw_q[...], gains[0])
    own[1] = rms_rows(raw_k[...], gains[1])
    for i, (dx, dl, dy) in enumerate(cube):
        block = own.at[:, :, columns_of(flip(x, dx) * SPLIT + group_at(dl, dy))]
        if i == 0:
            place(block, fresh_rows.at[:, my_rows])
        else:
            send(
                block, fresh_rows.at[:, my_rows], fresh_send.at[i], fresh_recv.at[i],
                (patch_at(0, dl, dy), flip(x, dx)),
            )

    @pl.when(low == high)
    def _():
        for copy in far:
            copy.start()

    cache_rows = rows_of(x, half_rows)
    side = pl.ds(pl.multiple_of(x * width_dev, width_dev), width_dev)
    other_side = pl.ds(pl.multiple_of((1 - x) * width_dev, width_dev), width_dev)
    place(own.at[1, :, side], key_cache.at[cache_rows])
    send(
        own.at[1, :, other_side], key_cache.at[cache_rows],
        cache_send.at[0], cache_recv.at[0], (patch, 1 - x),
    )
    for copy in local[5:]:
        copy.wait()

    for i, (dx, dl, dy) in enumerate(cube):
        if i > 0:
            arrive(
                fresh_rows.at[:, rows_of(group_at(dl, dy) * 2 + flip(x, dx), half_rows)],
                fresh_send.at[i], fresh_recv.at[i], (patch_at(0, dl, dy), flip(x, dx)),
            )

    factor = HD ** (-0.5) * 1.4426950408889634
    state = [None] * heads
    row_patch = lax.broadcasted_iota(jnp.int32, (chunk, 1), 0) // patch_rows
    column_patch = lax.broadcasted_iota(jnp.int32, (1, chunk), 1) // patch_rows

    def attend(h, keys, values, masked):
        columns = slice(h * HD, (h + 1) * HD)
        scores = lax.dot_general(
            fresh_rows[0, :, columns], keys[:, columns], (((1,), (1,)), ((), ())),
            preferred_element_type=jnp.float32,
        )
        if masked is not None:
            scores = jnp.where(masked, 2.0 * LOWEST, scores)
        new_max = jnp.max(scores, axis=1, keepdims=True)
        if state[h] is not None:
            row_max, row_sum, weighted = state[h]
            new_max = jnp.maximum(row_max, new_max)
        weights = jnp.exp2((scores - new_max) * factor)
        new_sum = jnp.sum(weights, axis=1, keepdims=True)
        added = jnp.dot(
            weights.astype(jnp.bfloat16), values[:, columns], preferred_element_type=jnp.float32
        )
        if state[h] is not None:
            rescale = jnp.exp2((row_max - new_max) * factor)
            new_sum += row_sum * rescale
            added += weighted * rescale
        state[h] = (new_max, new_sum, added)

    def give_back(h):
        _, row_sum, weighted = state[h]
        columns = slice(h * HD, (h + 1) * HD)
        result[:, columns] = (weighted / row_sum).astype(jnp.bfloat16)
        for i, (dx, dl, dy) in enumerate(cube):
            block = result.at[rows_of(group_at(dl, dy) * 2 + flip(x, dx), half_rows), columns]
            target = attended.at[:, head_columns(0, 0, 0, h)]
            if i == 0:
                place(block, target)
            else:
                send(
                    block, target, out_send.at[h, i], out_recv.at[h, i],
                    (patch_at(0, dl, dy), flip(x, dx)),
                )

    for h in range(heads):
        attend(h, fresh_rows.at[1], fresh_rows.at[2], row_patch != column_patch)

    for dh, dl in ((0, 0), (0, 1), (1, 0), (1, 1)):
        for i in range(8):
            if i > 0 and plane[i][:2] == (dh, dl):
                rows = key_rows_of(flip(high, dh), flip(low, dl), core, flip(y, plane[i][2]))
                for t in range(2):
                    arrive(
                        stale_rows.at[t, rows], stale_send.at[t, i], stale_recv.at[t, i],
                        (patch_at(*plane[i]), x),
                    )
        step = dh * 2 + dl
        block = flip(high, dh) * 2 + flip(low, dl)
        rows = rows_of(block * 2 + core, 2 * patch_rows)
        send(
            stale_rows.at[:, rows], stale_rows.at[:, rows],
            pass_send.at[step], pass_recv.at[step], sibling,
        )
        rows = rows_of(block * 2 + 1 - core, 2 * patch_rows)
        arrive(stale_rows.at[:, rows], pass_send.at[step], pass_recv.at[step], sibling)
        block = rows_of(block, chunk)
        masked = None
        if dh == 0:
            row_key = jnp.where(row_patch // 2 == flip(low, dl), row_patch % 2, -1)
            column_key = jnp.where(column_patch // 2 == core, column_patch % 2, -2)
            masked = row_key == column_key
        for h in range(heads):
            attend(h, stale_rows.at[0, block], stale_rows.at[1, block], masked)
            if (dh, dl) == (1, 1):
                give_back(h)

    for copy in started:
        copy.wait_send()
    arrive(key_cache.at[rows_of(1 - x, half_rows)], cache_send.at[0], cache_recv.at[0], (patch, 1 - x))
    for h in range(heads):
        for i, (dx, dl, dy) in enumerate(cube):
            if i > 0:
                arrive(
                    attended.at[:, head_columns(dx, dl, dy, h)],
                    out_send.at[h, i], out_recv.at[h, i], (patch_at(0, dl, dy), flip(x, dx)),
                )
    for copy in local[-heads:]:
        copy.wait()


def kernel_body(fresh_q, fresh_k, fresh_v, stale_k, stale_v, q_gain, k_gain):
    half_rows, width_all = fresh_q.shape
    patch_rows, width_dev = stale_k.shape
    tokens = patch_rows * lax.axis_size("patch")
    width = width_dev // SPLIT
    group = (SPLIT * patch_rows, width)
    bf16 = jnp.bfloat16
    in_hbm = pl.BlockSpec(memory_space=pltpu.HBM)
    sems = [(8,), (8,), (2, 8), (2, 8), (4,), (4,)]
    heads = width // HD
    sems += [(heads, 8), (heads, 8), (1,), (1,), (9 + heads,)]
    pairs = (width_dev // HD) * patch_rows * tokens
    return pl.pallas_call(
        kernel,
        out_shape=[
            jax.ShapeDtypeStruct((half_rows, width_all), bf16),
            jax.ShapeDtypeStruct((patch_rows, width_dev), bf16),
        ],
        in_specs=[in_hbm] * 7,
        out_specs=[in_hbm] * 2,
        scratch_shapes=[
            pltpu.VMEM((half_rows, width_all), bf16),
            pltpu.VMEM((half_rows, width_all), bf16),
            pltpu.VMEM((2, 1, width_all), jnp.float32),
            pltpu.VMEM((3, half_rows, width_all), bf16),
            pltpu.VMEM((3,) + group, bf16),
            pltpu.VMEM((2, tokens, width), bf16),
            pltpu.VMEM(group, bf16),
        ]
        + [pltpu.SemaphoreType.DMA(shape) for shape in sems],
        compiler_params=pltpu.CompilerParams(
            collective_id=0, has_side_effects=True, vmem_limit_bytes=62 * 1024 * 1024
        ),
        cost_estimate=pl.CostEstimate(
            flops=4 * pairs * HD, bytes_accessed=8 * tokens * width, transcendentals=pairs
        ),
    )(fresh_q, fresh_k, fresh_v, stale_k, stale_v, q_gain[None, :], k_gain[None, :])


def solution(mesh):
    placed = (
        P(("patch", "head"), None),
        P(("patch", "head"), None),
        P(("patch", "head"), None),
        P("patch", "head"),
        P("patch", "head"),
        P(),
        P(),
    )
    fits = mesh.shape["patch"] == 16 and mesh.shape["head"] == 2
    return jax.shard_map(
        kernel_body if fits else body,
        mesh=mesh,
        in_specs=placed,
        out_specs=(P(("patch", "head"), None), P("patch", "head")),
        check_vma=False,
    )
```
